32 devices in a mesh: dp: 16 (over z, y, core), blk: 2 (over x).
Axes of the slice: x: 2, y: 2, z: 4, core: 2. Of those that a mesh axis runs over, the one named last changes fastest.
Arguments:
- chars: int32 [2048, 16], P('blk', 'dp'), may hold values from 0 to 26
- timesteps: int32 [16], P('dp'), may hold values from 0 to 999
- embed: bfloat16 [27, 512], replicated, may hold values from -6 to 6
- ln1_gain: bfloat16 [2, 512], replicated, may hold values from 0.25 to 1.75
- ln1_bias: bfloat16 [2, 512], replicated, may hold values from -3 to 3
- w_time: bfloat16 [2, 512, 512], replicated, may hold values from -0.25 to 0.25
- w_qkv: bfloat16 [2, 512, 1536], replicated, may hold values from -0.25 to 0.25
- w_out: bfloat16 [2, 512, 512], replicated, may hold values from -6 to 6
- ln2_gain: bfloat16 [2, 512], replicated, may hold values from 0.25 to 1.75
- ln2_bias: bfloat16 [2, 512], replicated, may hold values from -3 to 3
- expand_weight: bfloat16 [2, 512, 2048], replicated, may hold values from -0.25 to 0.25
- expand_bias: bfloat16 [2, 2048], replicated, may hold values from -3 to 3
- contract_weight: bfloat16 [2, 2048, 512], replicated, may hold values from -0.125 to 0.125
- cotangent: bfloat16 [2048, 16, 512], P('blk', 'dp'), may hold values from -6 to 6
Outputs:
- activations: bfloat16 [2048, 16, 512], P('blk', 'dp')
- embed_grad: float32 [27, 512], replicated
- ln1_gain_grad: float32 [2, 512], replicated
- ln1_bias_grad: float32 [2, 512], replicated
- time_grad: float32 [2, 512, 512], replicated
- qkv_grad: float32 [2, 512, 1536], replicated
- out_grad: float32 [2, 512, 512], replicated
- ln2_gain_grad: float32 [2, 512], replicated
- ln2_bias_grad: float32 [2, 512], replicated
- up_grad: float32 [2, 512, 2048], replicated
- up_bias_grad: float32 [2, 2048], replicated
- down_grad: float32 [2, 2048, 512], replicated
The draws below stay inside these ranges and needn't reach their ends.
All inputs are finite; a program needn't handle non-finite values.
Results may differ from the reference program's by a relative error of at most 0.015.
Values may be sent and summed in bfloat16 or wider, within the bound.
No kernel may reach another device: no remote copies, remote signals or barrier semaphores. Data moves between devices by JAX's collectives and lax.ppermute only.
A program may use at most 512 MiB of HBM per device.

```python
import math
import jax
import jax.numpy as jnp
from jax import lax

D = 512
HEADS = 8
HEAD = 64
FF = 2048
VOCAB = 27
STEPS = 1000
LAYERS = 2
LENGTH = 2048
SEQS = 16
N_DP = 16
N_BLK = 2


def plant(entries, own_key, least, largest):
    place = [jax.random.randint(jax.random.fold_in(own_key, axis), (), 0, length) for axis, length in enumerate(entries.shape)]
    widest = entries.shape.index(max(entries.shape))
    beside = place[:widest] + [(place[widest] + 1) % entries.shape[widest]] + place[widest + 1:]
    return entries.at[tuple(place)].set(least).at[tuple(beside)].set(largest)


def spiked(drawn, key, source, target, parts, factor):
    owner, partner = [(jnp.arange(drawn.shape[dim]) // (drawn.shape[dim] // parts)).reshape([-1 if axis == dim else 1 for axis in range(drawn.ndim)]) for dim in (source, target)]
    chosen = jax.random.permutation(key, parts)[partner]
    strong = (owner == chosen) | (owner == (partner + parts // 2) % parts)
    return jnp.where(strong, factor * drawn, drawn)


def block_scale(key, dims, shards, smallest, top_value):
    level = 1.0
    for axis_at, shards_of in shards:
        heights = jax.random.uniform(jax.random.fold_in(jax.random.fold_in(key, 6), axis_at), (shards_of,), jnp.float32, smallest / len(shards), top_value / len(shards))
        level = level * jnp.repeat(jnp.exp(heights), dims[axis_at] // shards_of).reshape((-1,) + (1,) * (len(dims) - 1 - axis_at))
    return level


def noise(rng, shape, spread, most, shards=(), kind=jnp.bfloat16):
    values = jax.random.normal(rng, shape, jnp.float32) * spread
    if len(shards) > 0:
        values = block_scale(rng, shape, shards, -0.22, 0.18) * values
    return jnp.clip(values, min=-most, max=most).astype(kind)


def heavy_noise(key, dims, deviation, most, split, heavy, kind=jnp.bfloat16):
    entries = deviation * jax.random.normal(key, dims, jnp.float32)
    if split:
        entries = entries * block_scale(key, dims, split, -0.22, 0.18)
    return jnp.clip(spiked(entries, jax.random.fold_in(key, 3), *heavy), -most, most).astype(kind)


def setup_inputs(seed: int = 0) -> dict:
    splits = jax.random.split(jax.random.key(seed), 15)
    chars = plant(jax.random.randint(splits[0], (LENGTH, SEQS), 0, VOCAB), jax.random.fold_in(splits[0], 1), 0, VOCAB - 1).astype(jnp.int32)
    timesteps = plant(jax.random.randint(splits[1], (SEQS,), 0, STEPS), jax.random.fold_in(splits[1], 1), 0, STEPS - 1).astype(jnp.int32)
    embed = noise(splits[2], (VOCAB, D), 1.0, 6.0)
    ln1_gain = jnp.clip(1.0 + 0.15 * jax.random.normal(splits[3], (LAYERS, D), jnp.float32), 0.25, 1.75).astype(jnp.bfloat16)
    ln1_bias = noise(splits[4], (LAYERS, D), 0.5, 3.0)
    w_time = noise(splits[5], (LAYERS, D, D), D ** -0.5, 0.25)
    w_qkv = noise(splits[6], (LAYERS, D, 3 * D), D ** -0.5, 0.25)
    w_out = noise(splits[7], (LAYERS, D, D), (4 * D // LENGTH) ** -0.5, 6.0)
    ln2_gain = jnp.clip(1.0 + 0.15 * jax.random.normal(splits[8], (LAYERS, D), jnp.float32), 0.25, 1.75).astype(jnp.bfloat16)
    ln2_bias = noise(splits[9], (LAYERS, D), 0.5, 3.0)
    expand_weight = noise(splits[10], (LAYERS, D, FF), D ** -0.5, 0.25)
    expand_bias = noise(splits[11], (LAYERS, FF), 0.5, 3.0)
    contract_weight = noise(splits[12], (LAYERS, FF, D), FF ** -0.5, 0.125)
    cotangent = heavy_noise(splits[13], (LENGTH, SEQS, D), 1.0, 6.0, ((0, 2), (1, 16)), (1, 2, 16, 2.0))
    return dict(chars=chars, timesteps=timesteps, embed=embed, ln1_gain=ln1_gain, ln1_bias=ln1_bias, w_time=w_time, w_qkv=w_qkv, w_out=w_out, ln2_gain=ln2_gain, ln2_bias=ln2_bias, expand_weight=expand_weight, expand_bias=expand_bias, contract_weight=contract_weight, cotangent=cotangent)


@jax.custom_vjp
def low(v):
    return lax.optimization_barrier(v.astype(jnp.bfloat16)).astype(jnp.float32)

@jax.custom_vjp
def reduced_pullback(v):
    return v

def low_keep(v):
    return (low(v), None)

def low_pass(kept, grad):
    return (grad,)

def back_keep(v):
    return (v, None)

def back_low(kept, grad):
    return (low(grad),)
low.defvjp(low_keep, low_pass)
reduced_pullback.defvjp(back_keep, back_low)

def time_features(timesteps, model_width):
    half_width = model_width // 2
    frequency = jnp.exp(jnp.arange(half_width, dtype=jnp.float32) * (-math.log(10000.0) / half_width))
    phases = timesteps.astype(jnp.float32)[:, None] * frequency[None, :]
    return jnp.concatenate([jnp.sin(phases), jnp.cos(phases)], axis=1)

def layer_norm(values, norm_gain, norm_shift):
    center_mean = lax.optimization_barrier(jnp.mean(values, axis=-1, keepdims=True))
    centered = values - center_mean
    variance = lax.optimization_barrier(jnp.mean(centered * centered, axis=-1, keepdims=True))
    return centered * lax.rsqrt(variance + 1e-05) * norm_gain + norm_shift

def by_heads(matrix):
    return matrix.reshape(matrix.shape[0], HEADS, HEAD)

def attend_sequence(operands):
    queries, keys, values = operands
    exact_precision = lax.Precision.HIGHEST
    scores = reduced_pullback(jnp.einsum('qhe,khe->hqk', by_heads(queries), by_heads(keys), precision=exact_precision))
    row_max = lax.optimization_barrier(jnp.max(scores, axis=-1, keepdims=True))
    exponent = jnp.exp(scores - row_max)
    probability = low(exponent / lax.optimization_barrier(jnp.sum(exponent, axis=-1, keepdims=True)))
    mixture = jnp.einsum('hqk,khe->qhe', probability, by_heads(values), precision=exact_precision)
    return mixture.reshape(queries.shape[0], HEADS * HEAD)

def forward(chars, timesteps, embed, ln1_gain, ln1_bias, w_time, w_qkv, w_out, ln2_gain, ln2_bias, expand_weight, expand_bias, contract_weight):
    exact_precision = lax.Precision.HIGHEST
    residual_stream = embed[chars]
    features = low(time_features(timesteps, D))
    for layer_number in range(LAYERS):
        time_shift = jnp.dot(features, w_time[layer_number], precision=exact_precision)
        normed_in = residual_stream + time_shift[None, :, :]
        normed = low(layer_norm(normed_in, ln1_gain[layer_number], ln1_bias[layer_number]))
        projected = jnp.einsum('lsd,de->lse', normed, w_qkv[layer_number], precision=exact_precision)
        queries = low(reduced_pullback(projected[..., :D] * 0.125))
        keys = low(reduced_pullback(projected[..., D:2 * D]))
        values = low(reduced_pullback(projected[..., 2 * D:]))
        attended = lax.map(jax.checkpoint(attend_sequence), (queries.transpose(1, 0, 2), keys.transpose(1, 0, 2), values.transpose(1, 0, 2)))
        attended = low(reduced_pullback(attended.transpose(1, 0, 2)))
        middle_stream = normed_in + reduced_pullback(jnp.einsum('lsd,de->lse', attended, w_out[layer_number], precision=exact_precision))
        second_normalized = low(layer_norm(middle_stream, ln2_gain[layer_number], ln2_bias[layer_number]))
        expand_projected = reduced_pullback(jnp.einsum('gpo,ou->gpu', second_normalized, expand_weight[layer_number], precision=exact_precision) + expand_bias[layer_number])
        hidden_activation = low(jax.nn.gelu(expand_projected, approximate=False))
        residual_stream = middle_stream + reduced_pullback(jnp.einsum('weo,ok->wek', hidden_activation, contract_weight[layer_number], precision=exact_precision))
    return residual_stream

def reference(chars, timesteps, embed, ln1_gain, ln1_bias, w_time, w_qkv, w_out, ln2_gain, ln2_bias, expand_weight, expand_bias, contract_weight, cotangent):
    weights = tuple((weight.astype(jnp.float32) for weight in (embed, ln1_gain, ln1_bias, w_time, w_qkv, w_out, ln2_gain, ln2_bias, expand_weight, expand_bias, contract_weight)))

    def run_forward(*weight_list):
        return forward(chars, timesteps, *weight_list)
    residual_stream, pull_back = jax.vjp(run_forward, *weights)
    gradients = pull_back(cotangent.astype(jnp.float32))
    mean_scale = 1.0 / (N_DP * N_BLK)
    return (residual_stream.astype(jnp.bfloat16), gradients[0] * mean_scale, gradients[1] * mean_scale, gradients[2] * mean_scale, gradients[3] * mean_scale, gradients[4] * mean_scale, gradients[5] * mean_scale, gradients[6] * mean_scale, gradients[7] * mean_scale, gradients[8] * mean_scale, gradients[9] * mean_scale, gradients[10] * mean_scale)
```

```python
import math

import jax
import jax.numpy as jnp
from jax import lax
from jax.sharding import PartitionSpec as P

HEADS = 8
ROWS = 32
BF = jnp.bfloat16
F32 = jnp.float32


def mm(a, b, spec):
    return jnp.einsum(spec, a.astype(BF), b.astype(BF), preferred_element_type=F32)


def time_features(timesteps, model_width):
    half_width = model_width // 2
    frequency = jnp.exp(
        jnp.arange(half_width, dtype=F32) * (-math.log(10000.0) / half_width)
    )
    phases = timesteps.astype(F32)[:, None] * frequency[None, :]
    return jnp.concatenate([jnp.sin(phases), jnp.cos(phases)], axis=1).astype(BF)


def norm_parts(values):
    mean = jnp.mean(values, axis=-1, keepdims=True)
    centered = values - mean
    rstd = lax.rsqrt(jnp.mean(centered * centered, axis=-1, keepdims=True) + 1e-05)
    return centered * rstd, rstd


def norm_back(grad_out, unit, rstd, gain):
    scaled = grad_out * gain
    return rstd * (
        scaled
        - jnp.mean(scaled, axis=-1, keepdims=True)
        - unit * jnp.mean(scaled * unit, axis=-1, keepdims=True)
    )


def per_device(
    chars,
    timesteps,
    embed,
    ln1_gain,
    ln1_bias,
    w_time,
    w_qkv,
    w_out,
    ln2_gain,
    ln2_bias,
    expand_weight,
    expand_bias,
    contract_weight,
    cotangent,
):
    vocab, width = embed.shape
    layers = w_qkv.shape[0]
    heads, head = HEADS, width // HEADS
    scale = 1.0 / (lax.axis_size("dp") * lax.axis_size("blk"))
    local_seqs = chars.shape[1]
    onehot = (chars[:, :, None] == jnp.arange(ROWS, dtype=jnp.int32)).astype(BF)
    counts = jnp.sum(onehot.astype(F32), axis=0)
    sums = mm(onehot, cotangent, "psc,psd->scd")
    counts = lax.psum(counts, "blk")
    sums = lax.psum(sums, "blk")
    counts = lax.all_gather(counts, "dp", axis=0, tiled=True)
    times = lax.all_gather(timesteps, "dp", axis=0, tiled=True)
    grad = lax.all_gather(sums, "dp", axis=0, tiled=True)
    seqs = counts.shape[0]
    rows = seqs * ROWS

    features = time_features(times, width)
    stream = jnp.broadcast_to(
        jnp.pad(embed.astype(F32), ((0, ROWS - vocab), (0, 0)))[None], (seqs, ROWS, width)
    )
    present = (counts > 0)[:, None, None, :]
    weight_of = counts[:, None, None, :]
    saved = []
    for layer in range(layers):
        shift = mm(features, w_time[layer], "sd,de->se")
        normed_in = stream + shift[:, None, :]
        unit_one, rstd_one = norm_parts(normed_in)
        normed = (unit_one * ln1_gain[layer] + ln1_bias[layer]).astype(BF)
        projected = mm(normed, w_qkv[layer], "scd,de->sce")
        queries, keys, values = (
            part.reshape(seqs, ROWS, heads, head).astype(BF)
            for part in (
                projected[..., :width] * 0.125,
                projected[..., width : 2 * width],
                projected[..., 2 * width :],
            )
        )
        scores = mm(queries, keys, "sqhe,skhe->shqk")
        row_max = jnp.max(jnp.where(present, scores, -jnp.inf), axis=-1, keepdims=True)
        weighted = jnp.where(present, jnp.exp(jnp.minimum(scores - row_max, 0.0)), 0.0) * weight_of
        probs = weighted / jnp.sum(weighted, axis=-1, keepdims=True)
        attended = mm(probs, values, "shqk,skhe->sqhe").reshape(seqs, ROWS, width).astype(BF)
        middle = normed_in + mm(attended, w_out[layer], "scd,de->sce")
        unit_two, rstd_two = norm_parts(middle)
        normed_two = (unit_two * ln2_gain[layer] + ln2_bias[layer]).astype(BF)
        up = mm(normed_two, expand_weight[layer], "scd,df->scf") + expand_bias[layer].astype(F32)
        phi = 0.5 * (1.0 + lax.erf(up * math.sqrt(0.5)))
        hidden = (up * phi).astype(BF)
        slope = phi + up * jnp.exp(-0.5 * up * up) * (1.0 / math.sqrt(2 * math.pi))
        stream = middle + mm(hidden, contract_weight[layer], "scf,fd->scd")
        saved.append(
            (unit_one, rstd_one, normed, queries, keys, values, probs, attended, unit_two, rstd_two,
             normed_two, hidden, slope)
        )
    own = lax.axis_index("dp") * local_seqs
    table = lax.dynamic_slice_in_dim(stream.astype(BF), own, local_seqs, axis=0)
    activations = mm(onehot, table, "psc,scd->psd").astype(BF)

    per_layer = [None] * layers
    for layer in reversed(range(layers)):
        (unit_one, rstd_one, normed, queries, keys, values, probs, attended, unit_two, rstd_two,
         normed_two, hidden, slope) = saved[layer]
        down_term = mm(hidden, grad, "scf,scd->fd")
        grad_up = mm(grad, contract_weight[layer], "scd,fd->scf") * slope
        up_bias_term = jnp.sum(grad_up, axis=(0, 1))
        up_term = mm(normed_two, grad_up, "scd,scf->df")
        grad_normed_two = mm(grad_up, expand_weight[layer], "scf,df->scd")
        gain_two_term = jnp.sum(grad_normed_two * unit_two, axis=(0, 1))
        bias_two_term = jnp.sum(grad_normed_two, axis=(0, 1))
        grad_middle = grad + norm_back(grad_normed_two, unit_two, rstd_two, ln2_gain[layer].astype(F32))
        out_term = mm(attended, grad_middle, "scd,sce->de")
        grad_attended = mm(grad_middle, w_out[layer], "sce,de->scd").reshape(seqs, ROWS, heads, head)
        grad_probs = mm(grad_attended, values, "sqhe,skhe->shqk")
        delta = jnp.sum(probs * grad_probs, axis=-1, keepdims=True)
        grad_scores = probs * (grad_probs - delta)
        grad_queries = mm(grad_scores, keys, "shqk,skhe->sqhe") * 0.125
        grad_keys = mm(grad_scores, queries, "shqk,sqhe->skhe")
        grad_values = mm(probs, grad_attended, "shqk,sqhe->skhe")
        grad_projected = jnp.concatenate(
            [part.reshape(seqs, ROWS, width).astype(BF) for part in (grad_queries, grad_keys, grad_values)],
            axis=-1,
        )
        qkv_term = mm(normed, grad_projected, "scd,sce->de")
        grad_normed = mm(grad_projected, w_qkv[layer], "sce,de->scd")
        gain_one_term = jnp.sum(grad_normed * unit_one, axis=(0, 1))
        bias_one_term = jnp.sum(grad_normed, axis=(0, 1))
        grad = grad_middle + norm_back(grad_normed, unit_one, rstd_one, ln1_gain[layer].astype(F32))
        time_term = mm(features, jnp.sum(grad, axis=1), "sd,se->de")
        per_layer[layer] = [
            gain_one_term, bias_one_term, time_term, qkv_term, out_term, gain_two_term, bias_two_term,
            up_term, up_bias_term, down_term,
        ]
    embed_grad = jnp.sum(grad, axis=0)[:vocab] * scale
    stacked = [
        jnp.stack([per_layer[layer][member] for layer in range(layers)]) * scale
        for member in range(10)
    ]
    return (activations, embed_grad, *stacked)


def solution(mesh):
    in_specs = (P("blk", "dp"), P("dp")) + (P(),) * 11 + (P("blk", "dp", None),)
    out_specs = (P("blk", "dp", None),) + (P(),) * 11
    return jax.shard_map(
        per_device, mesh=mesh, in_specs=in_specs, out_specs=out_specs, check_vma=False
    )
```

```python
import math

import jax
import jax.numpy as jnp
from jax import lax
from jax.experimental import pallas as pl
from jax.experimental.pallas import tpu as pltpu
from jax.sharding import PartitionSpec as P

HEADS = 8
HEAD = 64
ROWS = 28
GROUP = 4
GROWS = ROWS * GROUP
CHUNK = 16
NROWS = ROWS * CHUNK
NGROUPS = CHUNK // GROUP
KPAD = 128
SLOT = 32
COUNT_ROW = 28
PIECE = 512
RBLOCK = 112
SPLIT = 32.0
MASKED = -1e30
BF = jnp.bfloat16
F32 = jnp.float32
I32 = jnp.int32
VMEM_BYTES = 60 * 2**20


def nn(a, b):
    return lax.dot_general(a, b, (((1,), (0,)), ((), ())), preferred_element_type=F32)


def nt(a, b):
    return lax.dot_general(a, b, (((1,), (1,)), ((), ())), preferred_element_type=F32)


def tn(a, b):
    return lax.dot_general(a, b, (((0,), (0,)), ((), ())), preferred_element_type=F32)


def iota(shape, dim):
    return lax.broadcasted_iota(I32, shape, dim)


def hi_lo(values):
    high = values.astype(BF)
    return high, (values - high.astype(F32)).astype(BF)


def row_seq(index):
    return lax.shift_right_logical(index * (65536 // ROWS + 1), 16)


def local_sums(chars_ref, cot_ref, place_ref, time_ref, out_ref):
    positions = chars_ref.shape[1]
    chars = chars_ref[...]
    onehot = (chars == iota((SLOT, positions), 0)).astype(F32).astype(BF)
    out_ref[...] = nn(onehot, cot_ref[...])
    placed = (chars + place_ref[0] * ROWS == iota((KPAD, positions), 0)).astype(F32).astype(BF)
    counts = nt(jnp.ones((8, positions), BF), placed)
    out_ref[COUNT_ROW : COUNT_ROW + 1, 0:KPAD] = counts[0:1]
    out_ref[COUNT_ROW : COUNT_ROW + 1, KPAD : 2 * KPAD] = jnp.full(
        (1, KPAD), time_ref[0].astype(F32) * time_ref[1].astype(F32) * (1.0 / 1024.0), F32
    )


def normalise(values):
    mean = jnp.mean(values, axis=-1, keepdims=True)
    centered = values - mean
    rstd = lax.rsqrt(jnp.mean(centered * centered, axis=-1, keepdims=True) + 1e-05)
    return centered * rstd, rstd


def norm_back(grad_out, unit, rstd, gain):
    scaled = grad_out * gain
    return rstd * (
        scaled
        - jnp.mean(scaled, axis=-1, keepdims=True)
        - unit * jnp.mean(scaled * unit, axis=-1, keepdims=True)
    )


def gelu_and_slope(up):
    size = jnp.abs(up)
    ratio = 1.0 / (1.0 + (0.3275911 * math.sqrt(0.5)) * size)
    bell = jnp.exp(-0.5 * (up * up))
    poly = 0.5 * 1.061405429
    for term in (-1.453152027, 1.421413741, -0.284496736, 0.254829592):
        poly = poly * ratio + 0.5 * term
    tail = poly * ratio * bell
    phi = jnp.where(up > 0, 1.0 - tail, tail)
    return up * phi, phi + (1.0 / math.sqrt(2 * math.pi)) * (up * bell)


def mega(
    own_ref, chars_ref, table_ref, embed_ref, g1_ref, b1_ref, g2_ref, b2_ref, eb_ref,
    wt_hbm, wq_hbm, wo_hbm, we_hbm, wc_hbm,
    act_ref, eg_ref, g1g_ref, b1g_ref, g2g_ref, b2g_ref, ubg_ref,
    tg_hbm, qg_hbm, og_hbm, ug_hbm, dg_hbm,
    wt, wq, wo, we, wc,
    unit1, rstd1, norm1, qkv, probs, att, unit2, rstd2, norm2, hid, slp,
    xs, mid, acc, bias, ga, gproj, gu, gb,
    tstage, qstage, ostage, ustage, dstage,
    in_sem, out_sem,
    *, scale, vocab,
):
    layers, width = g1_ref.shape
    inner = eb_ref.shape[1]
    pairs = width // 128
    pieces = inner // PIECE

    def fetch(index, source, target, layer):
        copy = pltpu.make_async_copy(source.at[layer], target.at[layer], in_sem.at[index, layer])
        copy.start()
        return copy

    loads = {}
    for layer in range(layers):
        for index, (name, source, target) in enumerate(
            (("t", wt_hbm, wt), ("q", wq_hbm, wq), ("o", wo_hbm, wo), ("e", we_hbm, we), ("c", wc_hbm, wc))
        ):
            loads[name, layer] = fetch(index, source, target, layer)

    row = iota((NROWS, 1), 0)
    seq_of = row_seq(row)
    char_of = row - seq_of * ROWS
    pick_char = (char_of == iota((NROWS, SLOT), 1)).astype(F32).astype(BF)
    pick_seq = (seq_of == iota((NROWS, CHUNK), 1)).astype(F32).astype(BF)

    stamp = []
    for group in range(NGROUPS):
        total = jnp.zeros((1, KPAD), F32)
        for member in range(GROUP):
            tail = table_ref[group * GROUP + member, SLOT - 16 : SLOT, 0 : 2 * KPAD].astype(F32)
            start = COUNT_ROW - (SLOT - 16)
            value = tail[start : start + 1] + SPLIT * tail[start + 1 : start + 2]
            total = total + value[:, 0:KPAD]
            stamp.append(value[:, KPAD:])
        column = iota((GROWS, KPAD), 1)
        same = row_seq(column) == row_seq(iota((GROWS, KPAD), 0))
        live = same & (column < GROWS) & (total > 0.5)
        bias[group] = jnp.where(live, jnp.log(jnp.maximum(total, 1.0)), MASKED)
    times = jnp.concatenate(stamp, axis=0)
    half = width // 2
    cycles = [
        times * jnp.exp((iota((1, KPAD), 1) + start).astype(F32) * (-math.log(10000.0) / half))
        for start in range(0, half, KPAD)
    ]
    features = jnp.concatenate(
        [jnp.sin(phase) for phase in cycles] + [jnp.cos(phase) for phase in cycles], axis=1
    ).astype(BF)

    left = (iota((KPAD, KPAD), 1) < HEAD).astype(F32)
    left_mask, right_mask = left.astype(BF), (1.0 - left).astype(BF)
    left_lanes = iota((GROWS, KPAD), 1) < HEAD
    for layer in range(layers):
        qkv[layer, NROWS:, :] = jnp.zeros((qkv.shape[1] - NROWS, qkv.shape[2]), BF)

    def blocks(layer, group, pair, part):
        lanes = part * width + pair * KPAD
        both = qkv[layer, group * GROWS : group * GROWS + KPAD, lanes : lanes + KPAD]
        return jnp.concatenate([both * left_mask, both * right_mask], axis=0)

    for layer in range(layers):
        loads["t", layer].wait()
        shift = nn(features, wt[layer])
        high, low = hi_lo(shift)
        shifted = nn(pick_seq, high) + nn(pick_seq, low)
        if layer == 0:
            xs[...] = nn(pick_char[:, 0:vocab], embed_ref[...]) + shifted
        else:
            xs[...] = xs[...] + shifted
        for start in range(0, NROWS, RBLOCK):
            span = slice(start, start + RBLOCK)
            unit, rstd = normalise(xs[span, :])
            unit1[layer, span, :] = unit.astype(BF)
            rstd1[layer, span, :] = jnp.broadcast_to(rstd, (RBLOCK, KPAD))
            norm1[layer, span, :] = (
                unit * g1_ref[layer : layer + 1, :].astype(F32) + b1_ref[layer : layer + 1, :].astype(F32)
            ).astype(BF)
        loads["q", layer].wait()
        qkv[layer, 0:NROWS, 0:width] = (nn(norm1[layer], wq[layer, :, 0:width]) * 0.125).astype(BF)
        qkv[layer, 0:NROWS, width:] = nn(norm1[layer], wq[layer, :, width:]).astype(BF)
        for group in range(NGROUPS):
            span = slice(group * GROWS, (group + 1) * GROWS)
            for pair in range(pairs):
                lanes = slice(pair * KPAD, (pair + 1) * KPAD)
                scores = nt(qkv[layer, span, lanes], blocks(layer, group, pair, 1))
                parts = []
                for side in range(2):
                    score = scores[:, side * KPAD : (side + 1) * KPAD] + bias[group]
                    weight = jnp.exp(score - jnp.max(score, axis=-1, keepdims=True))
                    parts.append((weight * (1.0 / jnp.sum(weight, axis=-1, keepdims=True))).astype(BF))
                prob = jnp.concatenate(parts, axis=1)
                probs[layer, span, 2 * pair * KPAD : 2 * (pair + 1) * KPAD] = prob
                att[layer, span, lanes] = nn(prob, blocks(layer, group, pair, 2)).astype(BF)
        loads["o", layer].wait()
        mid[...] = xs[...] + nn(att[layer], wo[layer])
        for start in range(0, NROWS, RBLOCK):
            span = slice(start, start + RBLOCK)
            unit, rstd = normalise(mid[span, :])
            unit2[layer, span, :] = unit.astype(BF)
            rstd2[layer, span, :] = jnp.broadcast_to(rstd, (RBLOCK, KPAD))
            norm2[layer, span, :] = (
                unit * g2_ref[layer : layer + 1, :].astype(F32) + b2_ref[layer : layer + 1, :].astype(F32)
            ).astype(BF)
        loads["e", layer].wait()
        loads["c", layer].wait()
        for piece in range(pieces):
            cols = slice(piece * PIECE, (piece + 1) * PIECE)
            up = nn(norm2[layer], we[layer, :, cols]) + eb_ref[layer : layer + 1, cols].astype(F32)
            hidden, slope = gelu_and_slope(up)
            hid[layer, :, cols] = hidden.astype(BF)
            slp[layer, :, cols] = slope.astype(BF)
        xs[...] = mid[...] + nn(hid[layer], wc[layer])

    own = own_ref[0]
    gb[0:NROWS, :] = xs[...].astype(BF)
    gb[NROWS:, :] = jnp.zeros((gb.shape[0] - NROWS, width), BF)
    place = chars_ref[...] + (own % GROUP) * ROWS
    hot = (place == iota((KPAD, chars_ref.shape[1]), 0)).astype(F32).astype(BF)
    act_ref[...] = tn(
        hot, gb[pl.ds(pl.multiple_of((own // GROUP) * GROWS, 16), KPAD), :]
    ).astype(BF)

    slot_row = seq_of * SLOT + char_of
    spread = (slot_row == iota((NROWS, CHUNK * SLOT), 1)).astype(F32).astype(BF)
    xs[...] = nn(spread, table_ref[...].reshape(CHUNK * SLOT, width)) * scale

    sends = {}

    def send(index, source, target, layer, value):
        if index in sends:
            sends.pop(index).wait()
        source[...] = value
        copy = pltpu.make_async_copy(source, target.at[layer], out_sem.at[index, layer])
        copy.start()
        sends[index] = copy

    for layer in reversed(range(layers)):
        grad_ff = xs[...].astype(BF)
        send(0, dstage, dg_hbm, layer, tn(hid[layer], grad_ff))
        for piece in range(pieces):
            cols = slice(piece * PIECE, (piece + 1) * PIECE)
            grad_up = nt(grad_ff, wc[layer, cols, :]) * slp[layer, :, cols].astype(F32)
            ubg_ref[layer : layer + 1, cols] = jnp.sum(grad_up, axis=0, keepdims=True)
            gu[:, cols] = grad_up.astype(BF)
        send(1, ustage, ug_hbm, layer, tn(norm2[layer], gu[...]))
        acc[...] = nt(gu[...], we[layer])
        gain_total = jnp.zeros((1, width), F32)
        bias_total = jnp.zeros((1, width), F32)
        for start in range(0, NROWS, RBLOCK):
            span = slice(start, start + RBLOCK)
            unit = unit2[layer, span, :].astype(F32)
            grad_norm = acc[span, :]
            gain_total += jnp.sum(grad_norm * unit, axis=0, keepdims=True)
            bias_total += jnp.sum(grad_norm, axis=0, keepdims=True)
            grad_mid = xs[span, :] + norm_back(
                grad_norm, unit, rstd2[layer, span, 0:1], g2_ref[layer : layer + 1, :].astype(F32)
            )
            mid[span, :] = grad_mid
            gb[span, :] = grad_mid.astype(BF)
        g2g_ref[layer : layer + 1, :] = gain_total
        b2g_ref[layer : layer + 1, :] = bias_total
        send(2, ostage, og_hbm, layer, tn(att[layer], gb[0:NROWS, :]))
        ga[...] = nt(gb[0:NROWS, :], wo[layer]).astype(BF)
        for group in range(NGROUPS):
            span = slice(group * GROWS, (group + 1) * GROWS)
            for pair in range(pairs):
                lanes = slice(pair * KPAD, (pair + 1) * KPAD)
                query = qkv[layer, span, lanes]
                keys, values = blocks(layer, group, pair, 1), blocks(layer, group, pair, 2)
                grad_att = ga[span, lanes]
                prob = probs[layer, span, 2 * pair * KPAD : 2 * (pair + 1) * KPAD]
                grad_prob = nt(grad_att, values)
                parts = []
                for side in range(2):
                    half_lanes = slice(side * KPAD, (side + 1) * KPAD)
                    weight, slope = prob[:, half_lanes].astype(F32), grad_prob[:, half_lanes]
                    delta = jnp.sum(weight * slope, axis=-1, keepdims=True)
                    parts.append((weight * (slope - delta)).astype(BF))
                grad_score = jnp.concatenate(parts, axis=1)
                gproj[span, lanes] = (nn(grad_score, keys) * 0.125).astype(BF)
                for part, product in ((1, tn(grad_score, query)), (2, tn(prob, grad_att))):
                    joined = jnp.where(left_lanes, product[0:GROWS], product[KPAD : KPAD + GROWS])
                    start = part * width + pair * KPAD
                    gproj[span, start : start + KPAD] = joined.astype(BF)
        send(3, qstage, qg_hbm, layer, tn(norm1[layer], gproj[...]))
        acc[...] = nt(gproj[...], wq[layer])
        gain_total = jnp.zeros((1, width), F32)
        bias_total = jnp.zeros((1, width), F32)
        for start in range(0, NROWS, RBLOCK):
            span = slice(start, start + RBLOCK)
            unit = unit1[layer, span, :].astype(F32)
            grad_norm = acc[span, :]
            gain_total += jnp.sum(grad_norm * unit, axis=0, keepdims=True)
            bias_total += jnp.sum(grad_norm, axis=0, keepdims=True)
            xs[span, :] = mid[span, :] + norm_back(
                grad_norm, unit, rstd1[layer, span, 0:1], g1_ref[layer : layer + 1, :].astype(F32)
            )
        g1g_ref[layer : layer + 1, :] = gain_total
        b1g_ref[layer : layer + 1, :] = bias_total
        high, low = hi_lo(xs[...])
        by_seq = tn(pick_seq, high) + tn(pick_seq, low)
        high_seq, low_seq = hi_lo(by_seq)
        send(4, tstage, tg_hbm, layer, tn(features, high_seq) + tn(features, low_seq))
        if layer == 0:
            eg_ref[...] = (tn(pick_char, high) + tn(pick_char, low))[0:vocab]
    for copy in sends.values():
        copy.wait()


def vmem():
    return pl.BlockSpec(memory_space=pltpu.VMEM)


def smem():
    return pl.BlockSpec(memory_space=pltpu.SMEM)


def anywhere():
    return pl.BlockSpec(memory_space=pl.ANY)


def run_chunk(own, chars_row, table, weights, scale):
    (embed, ln1_gain, ln1_bias, w_time, w_qkv, w_out, ln2_gain, ln2_bias, expand_weight, expand_bias,
     contract_weight) = weights
    layers, width = ln1_gain.shape
    inner = expand_bias.shape[1]
    vocab = embed.shape[0]
    padded = NROWS + KPAD - GROWS

    def f32_like(array):
        return jax.ShapeDtypeStruct(array.shape, F32)

    outs = pl.pallas_call(
        lambda *refs: mega(*refs, scale=scale, vocab=vocab),
        out_shape=[
            jax.ShapeDtypeStruct((chars_row.shape[1], width), BF),
            f32_like(embed), f32_like(ln1_gain), f32_like(ln1_bias), f32_like(ln2_gain),
            f32_like(ln2_bias), f32_like(expand_bias),
            f32_like(w_time), f32_like(w_qkv), f32_like(w_out), f32_like(expand_weight),
            f32_like(contract_weight),
        ],
        in_specs=[smem()] + [vmem()] * 8 + [anywhere()] * 5,
        out_specs=[vmem()] * 7 + [anywhere()] * 5,
        scratch_shapes=[
            pltpu.VMEM(w_time.shape, BF), pltpu.VMEM(w_qkv.shape, BF), pltpu.VMEM(w_out.shape, BF),
            pltpu.VMEM(expand_weight.shape, BF), pltpu.VMEM(contract_weight.shape, BF),
            pltpu.VMEM((layers, NROWS, width), BF),
            pltpu.VMEM((layers, NROWS, KPAD), F32),
            pltpu.VMEM((layers, NROWS, width), BF),
            pltpu.VMEM((layers, padded, 3 * width), BF),
            pltpu.VMEM((layers, NROWS, HEADS * KPAD), BF),
            pltpu.VMEM((layers, NROWS, width), BF),
            pltpu.VMEM((layers, NROWS, width), BF),
            pltpu.VMEM((layers, NROWS, KPAD), F32),
            pltpu.VMEM((layers, NROWS, width), BF),
            pltpu.VMEM((layers, NROWS, inner), BF),
            pltpu.VMEM((layers, NROWS, inner), BF),
            pltpu.VMEM((NROWS, width), F32),
            pltpu.VMEM((NROWS, width), F32),
            pltpu.VMEM((NROWS, width), F32),
            pltpu.VMEM((NGROUPS, GROWS, KPAD), F32),
            pltpu.VMEM((NROWS, width), BF),
            pltpu.VMEM((NROWS, 3 * width), BF),
            pltpu.VMEM((NROWS, inner), BF),
            pltpu.VMEM((padded, width), BF),
            pltpu.VMEM(w_time.shape[1:], F32), pltpu.VMEM(w_qkv.shape[1:], F32),
            pltpu.VMEM(w_out.shape[1:], F32), pltpu.VMEM(expand_weight.shape[1:], F32),
            pltpu.VMEM(contract_weight.shape[1:], F32),
            pltpu.SemaphoreType.DMA((5, layers)),
            pltpu.SemaphoreType.DMA((5, layers)),
        ],
        compiler_params=pltpu.CompilerParams(vmem_limit_bytes=VMEM_BYTES),
        name="tables",
    )(own, chars_row, table, embed, ln1_gain, ln1_bias, ln2_gain, ln2_bias, expand_bias,
      w_time, w_qkv, w_out, expand_weight, contract_weight)
    act, eg, g1, b1, g2, b2, ub, tg, qg, og, ug, dg = outs
    return act, (eg, g1, b1, tg, qg, og, g2, b2, ug, ub, dg)


def per_device(chars, timesteps, *rest):
    weights, cotangent = rest[:-1], rest[-1]
    width = weights[0].shape[1]
    n_dp, n_blk = lax.axis_size("dp"), lax.axis_size("blk")
    seq = lax.axis_index("dp")
    positions = chars.shape[0]
    chars_row = chars.reshape(1, positions)
    sums = pl.pallas_call(
        local_sums,
        out_shape=jax.ShapeDtypeStruct((SLOT, width), F32),
        in_specs=[vmem(), vmem(), smem(), smem()],
        out_specs=vmem(),
        compiler_params=pltpu.CompilerParams(vmem_limit_bytes=VMEM_BYTES),
        name="local_sums",
    )(
        chars_row,
        cotangent.reshape(positions, width),
        (seq % GROUP).astype(I32).reshape(1),
        jnp.stack([timesteps[0], jnp.int32(1024 // n_blk)]),
    )
    total = sums
    for step in range(1, n_blk):
        total = total + lax.ppermute(sums, "blk", [(i, (i + step) % n_blk) for i in range(n_blk)])
    numbers = total[COUNT_ROW : COUNT_ROW + 1]
    high = jnp.floor(numbers * (1.0 / SPLIT))
    block = jnp.concatenate(
        [total[:COUNT_ROW], numbers - SPLIT * high, high, jnp.zeros((SLOT - COUNT_ROW - 2, width), F32)]
    ).astype(BF)
    table = lax.all_to_all(
        jnp.broadcast_to(block[None], (n_dp, SLOT, width)), "dp", split_axis=0, concat_axis=0, tiled=True
    )
    scale = 1.0 / (n_dp * n_blk)
    if n_dp == CHUNK:
        act, grads = run_chunk(seq.reshape(1).astype(I32), chars_row, table, weights, scale)
    else:

        def step(carry, chunk):
            act, grads = carry
            place = seq - chunk * CHUNK
            inside = (place >= 0) & (place < CHUNK)
            part = lax.dynamic_slice_in_dim(table, chunk * CHUNK, CHUNK, axis=0)
            new_act, new_grads = run_chunk(
                jnp.clip(place, 0, CHUNK - 1).reshape(1).astype(I32), chars_row, part, weights, scale
            )
            return (jnp.where(inside, new_act, act), tuple(a + b for a, b in zip(grads, new_grads))), None

        start = (jnp.zeros((positions, width), BF), tuple(jnp.zeros(w.shape, F32) for w in weights))
        (act, grads), _ = lax.scan(step, start, jnp.arange(n_dp // CHUNK, dtype=I32))
    return (act.reshape(positions, 1, width), *grads)


def solution(mesh):
    in_specs = (P("blk", "dp"), P("dp")) + (P(),) * 11 + (P("blk", "dp", None),)
    out_specs = (P("blk", "dp", None),) + (P(),) * 11
    return jax.shard_map(
        per_device, mesh=mesh, in_specs=in_specs, out_specs=out_specs, check_vma=False
    )
```

```python
import math
from types import SimpleNamespace

import jax
import jax.numpy as jnp
from jax import lax
from jax.experimental import pallas as pl
from jax.experimental.pallas import tpu as pltpu
from jax.sharding import PartitionSpec as P

HEADS = 8
HEAD = 64
ROWS = 28
GROUP = 4
GROWS = ROWS * GROUP
CHUNK = 16
NROWS = ROWS * CHUNK
NGROUPS = CHUNK // GROUP
KPAD = 128
SLOT = 32
PIECE = 512
HALF = NROWS // 2
MASKED = -1e30
BF = jnp.bfloat16
F32 = jnp.float32
I32 = jnp.int32
MIB = 2**20
DEPTH = 3


def nn(a, b):
    return lax.dot_general(a, b, (((1,), (0,)), ((), ())), preferred_element_type=F32)


def nt(a, b):
    return lax.dot_general(a, b, (((1,), (1,)), ((), ())), preferred_element_type=F32)


def tn(a, b):
    return lax.dot_general(a, b, (((0,), (0,)), ((), ())), preferred_element_type=F32)


def iota(shape, dim):
    return lax.broadcasted_iota(I32, shape, dim)


def hi_lo(values):
    high = values.astype(BF)
    return high, (values - high.astype(F32)).astype(BF)


def row_seq(index):
    return lax.shift_right_logical(index * (65536 // ROWS + 1), 16)


def local_sums(chars_ref, cot_ref, place_ref, time_ref, count_ref, sum_ref, *, shares):
    positions = chars_ref.shape[1]
    chars = chars_ref[...]
    placed = (chars + place_ref[0] * ROWS == iota((KPAD, positions), 0)).astype(F32)
    counts = nt(jnp.ones((8, positions), BF), placed.astype(BF))[0:1]
    stamp = jnp.full((1, KPAD), time_ref[0].astype(F32) * (1.0 / shares), F32)
    row = jnp.concatenate([counts, stamp], axis=1)
    for device in range(count_ref.shape[0]):
        count_ref[device] = row
    onehot = (chars == iota((SLOT, positions), 0)).astype(F32)
    sum_ref[...] = nn(onehot.astype(BF), cot_ref[...])


def spread_sums(*refs):
    total = refs[0][...]
    for ref in refs[1:-1]:
        total = total + ref[...]
    total = total.astype(BF)
    for device in range(refs[-1].shape[0]):
        refs[-1][device] = total


class Loads:
    def __init__(self, depth):
        self.depth, self.queue, self.done = depth, [], set()

    def add(self, key, source, target, sem):
        self.queue.append((key, pltpu.make_async_copy(source, target, sem)))

    def begin(self):
        for _, copy in self.queue[: self.depth]:
            copy.start()
        self.started = min(self.depth, len(self.queue))

    def need(self, *keys):
        for key in keys:
            while key not in self.done:
                first, copy = self.queue[len(self.done)]
                copy.wait()
                self.done.add(first)
                if self.started < len(self.queue):
                    self.queue[self.started][1].start()
                    self.started += 1


def normalise(values):
    mean = jnp.mean(values, axis=-1, keepdims=True)
    centered = values - mean
    rstd = lax.rsqrt(jnp.mean(centered * centered, axis=-1, keepdims=True) + 1e-05)
    return centered * rstd, rstd


def norm_back(grad_out, unit, rstd, gain):
    scaled = grad_out * gain
    return rstd * (
        scaled
        - jnp.mean(scaled, axis=-1, keepdims=True)
        - unit * jnp.mean(scaled * unit, axis=-1, keepdims=True)
    )


def gelu_and_slope(up):
    size = jnp.abs(up)
    bell = jnp.exp2((-0.5 / math.log(2.0)) * (up * up))
    shift = math.sqrt(2.0) / 0.3275911
    ratio = 1.0 / (shift + size)
    poly = 0.5 * shift**5 * 1.061405429
    for power, term in ((4, -1.453152027), (3, 1.421413741), (2, -0.284496736), (1, 0.254829592)):
        poly = poly * ratio + 0.5 * shift**power * term
    tail = (poly * ratio) * bell
    slope = tail - (size * bell) * (1.0 / math.sqrt(2 * math.pi))
    return jnp.maximum(up, 0.0) - size * tail, jnp.where(up > 0, 1.0 - slope, slope)


def row_choices():
    row = iota((NROWS, 1), 0)
    seq_of = row_seq(row)
    char_of = row - seq_of * ROWS
    pick_char = (char_of == iota((NROWS, SLOT), 1)).astype(F32).astype(BF)
    pick_seq = (seq_of == iota((NROWS, CHUNK), 1)).astype(F32).astype(BF)
    return seq_of, char_of, pick_char, pick_seq


def side_masks():
    left = (iota((GROWS, KPAD), 1) < HEAD).astype(F32)
    return left.astype(BF), (1.0 - left).astype(BF)


def blocks(qkv, masks, group, pair, part):
    lanes = part * (qkv.shape[1] // 3) + pair * KPAD
    both = qkv[group * GROWS : (group + 1) * GROWS, lanes : lanes + KPAD]
    return jnp.concatenate([both * masks[0], both * masks[1]], axis=0)


def wide(ref, layer):
    return ref[layer : layer + 1, :].astype(F32)


KEPT = ("unit1", "rstd1", "norm1", "qkv", "probs", "att", "unit2", "rstd2", "norm2", "hid", "slp")


def kept_shapes(width, inner):
    row = {"rstd1": (KPAD, F32), "rstd2": (KPAD, F32), "qkv": (3 * width, BF), "hid": (inner, BF), "slp": (inner, BF)}
    shapes = {name: ((NROWS, row.get(name, (width, BF))[0]), row.get(name, (width, BF))[1]) for name in KEPT}
    shapes["probs"] = ((NGROUPS, HEADS // 2, 2 * GROWS, GROWS), BF)
    return [shapes[name] for name in KEPT]


def halves(size=HALF):
    return [slice(start, start + size) for start in range(0, NROWS, size)]


def groups_of(span):
    return range(span.start // GROWS, span.stop // GROWS)


def forward_tasks(layer, small, weight, kept, source, xs, mid, bias, masks, need):
    width = xs.shape[1]
    inner = kept.hid.shape[1]
    pairs = width // KPAD

    def normed(span, values, unit_ref, rstd_ref, norm_ref, gain, shift):
        unit, rstd = normalise(values[span, :])
        unit_ref[span, :] = unit.astype(BF)
        rstd_ref[span, :] = jnp.broadcast_to(rstd, (rstd.shape[0], KPAD))
        norm_ref[span, :] = (unit * wide(gain, layer) + wide(shift, layer)).astype(BF)

    def ln1(span):
        normed(span, source, kept.unit1, kept.rstd1, kept.norm1, small.g1, small.b1)

    def qkv(span):
        need("q")
        for part in range(3):
            lanes = slice(part * width, (part + 1) * width)
            product = nn(kept.norm1[span, :], weight.q[:, lanes])
            kept.qkv[span, lanes] = (product * 0.125 if part == 0 else product).astype(BF)

    def attend(span):
        for group in groups_of(span):
            rows = slice(group * GROWS, (group + 1) * GROWS)
            lanes = [slice(pair * KPAD, (pair + 1) * KPAD) for pair in range(pairs)]
            scores = [
                nt(blocks(kept.qkv, masks, group, pair, 1), kept.qkv[rows, lanes[pair]]) for pair in range(pairs)
            ]
            for pair in range(pairs):
                for side in range(2):
                    keys = slice(side * GROWS, (side + 1) * GROWS)
                    score = scores[pair][keys] + bias[group]
                    heft = jnp.exp(score - jnp.max(score, axis=0, keepdims=True))
                    prob = heft * (1.0 / jnp.sum(heft, axis=0, keepdims=True))
                    kept.probs[group, pair, keys, :] = prob.astype(BF)
            for pair in range(pairs):
                kept.att[rows, lanes[pair]] = tn(
                    kept.probs[group, pair], blocks(kept.qkv, masks, group, pair, 2)
                ).astype(BF)

    def out(span):
        need("o")
        mid[span, :] = source[span, :] + nn(kept.att[span, :], weight.o[...])

    def ln2(span):
        normed(span, mid, kept.unit2, kept.rstd2, kept.norm2, small.g2, small.b2)

    def up(span):
        need("e")
        for piece in range(inner // PIECE):
            cols = slice(piece * PIECE, (piece + 1) * PIECE)
            product = nn(kept.norm2[span, :], weight.e[:, cols])
            hidden, slope = gelu_and_slope(product + small.eb[layer : layer + 1, cols].astype(F32))
            kept.hid[span, cols] = hidden.astype(BF)
            kept.slp[span, cols] = slope.astype(BF)

    def down(span):
        need("c")
        xs[span, :] = mid[span, :] + nn(kept.hid[span, :], weight.c[...])

    parts = dict(ln1=ln1, qkv=qkv, attend=attend, out=out, ln2=ln2, up=up, down=down)
    return {
        f"{name}{half}": (lambda part=part, span=span: part(span))
        for name, part in parts.items()
        for half, span in enumerate(halves())
    }


def backward_tasks(layer, small, weight, kept, work, masks, need, send, features, picks, grads):
    xs, mid, acc = work.xs, work.mid, work.acc
    width = xs.shape[1]
    inner = kept.hid.shape[1]
    pairs = width // KPAD
    left_lanes = iota((GROWS, KPAD), 1) < HEAD

    def add_rows(ref, span, value, cols=slice(None)):
        total = jnp.sum(value, axis=0, keepdims=True)
        ref[layer : layer + 1, cols] = total if span.start == 0 else ref[layer : layer + 1, cols] + total

    def grad_up(span):
        need("c", "slp")
        for piece in range(inner // PIECE):
            cols = slice(piece * PIECE, (piece + 1) * PIECE)
            value = nt(work.gff[span, :], weight.c[cols, :]) * kept.slp[span, cols].astype(F32)
            add_rows(grads.ub, span, value, cols)
            work.gu[span, cols] = value.astype(BF)

    def grad_norm2(span):
        need("e")
        acc[span, :] = nt(work.gu[span, :], weight.e[...])

    def ln2_back(span):
        need("unit2", "rstd2")
        unit, grad = kept.unit2[span, :].astype(F32), acc[span, :]
        add_rows(grads.g2, span, grad * unit)
        add_rows(grads.b2, span, grad)
        total = xs[span, :] + norm_back(grad, unit, kept.rstd2[span, 0:1], wide(small.g2, layer))
        mid[span, :] = total
        work.gb[span, :] = total.astype(BF)

    def grad_att(span):
        need("o")
        work.ga[span, :] = nt(work.gb[span, :], weight.o[...]).astype(BF)

    def attend_back(span):
        need("qkv", "probs")
        for group in groups_of(span):
            rows = slice(group * GROWS, (group + 1) * GROWS)
            lanes = [slice(pair * KPAD, (pair + 1) * KPAD) for pair in range(pairs)]
            grad_probs = [
                nt(blocks(kept.qkv, masks, group, pair, 2), work.ga[rows, lanes[pair]]) for pair in range(pairs)
            ]
            for pair in range(pairs):
                for side in range(2):
                    keys = slice(side * GROWS, (side + 1) * GROWS)
                    prob = kept.probs[group, pair, keys, :].astype(F32)
                    grad_prob = grad_probs[pair][keys]
                    delta = jnp.sum(prob * grad_prob, axis=0, keepdims=True)
                    work.gscore[pair, keys, :] = (prob * (grad_prob - delta)).astype(BF)
            for pair in range(pairs):
                grad_score = work.gscore[pair]
                work.gproj[rows, lanes[pair]] = (
                    tn(grad_score, blocks(kept.qkv, masks, group, pair, 1)) * 0.125
                ).astype(BF)
                grad_key = nn(grad_score, kept.qkv[rows, lanes[pair]])
                grad_value = nn(kept.probs[group, pair], work.ga[rows, lanes[pair]])
                for part, product in ((1, grad_key), (2, grad_value)):
                    joined = jnp.where(left_lanes, product[0:GROWS], product[GROWS : 2 * GROWS])
                    start = part * width + pair * KPAD
                    work.gproj[rows, start : start + KPAD] = joined.astype(BF)

    def grad_norm1(span):
        need("q")
        acc[span, :] = nt(work.gproj[span, :], weight.q[...])

    def ln1_back(span):
        need("unit1", "rstd1")
        unit, grad = kept.unit1[span, :].astype(F32), acc[span, :]
        add_rows(grads.g1, span, grad * unit)
        add_rows(grads.b1, span, grad)
        total = mid[span, :] + norm_back(grad, unit, kept.rstd1[span, 0:1], wide(small.g1, layer))
        xs[span, :] = total
        work.gff[span, :] = total.astype(BF)

    def down_term():
        need("hid")
        send("down", layer, lambda: tn(kept.hid[...], work.gff[...]))

    def up_term():
        need("norm2")
        send("up", layer, lambda: tn(kept.norm2[...], work.gu[...]))

    def out_term():
        need("att")
        send("out", layer, lambda: tn(kept.att[...], work.gb[...]))

    def qkv_term():
        need("norm1")
        send("qkv", layer, lambda: tn(kept.norm1[...], work.gproj[...]))

    def time_term():
        pick_char, pick_seq = picks
        by_seq = tn(pick_seq, work.gff[...]).astype(BF)
        send("time", layer, lambda: tn(features, by_seq))
        if layer == 0:
            grads.eg[...] = tn(pick_char, work.gff[...])[0 : grads.eg.shape[0]]

    by_half = dict(
        grad_up=grad_up, grad_norm2=grad_norm2, ln2_back=ln2_back, grad_att=grad_att,
        attend_back=attend_back, grad_norm1=grad_norm1, ln1_back=ln1_back,
    )
    tasks = {
        f"{name}{half}": (lambda part=part, span=span: part(span))
        for name, part in by_half.items()
        for half, span in enumerate(halves(NROWS))
    }
    tasks.update(down_term=down_term, up_term=up_term, out_term=out_term, qkv_term=qkv_term, time_term=time_term)
    return tasks


FORWARD_ORDER = (
    "ln10", "ln11", "qkv0", "qkv1", "attend0", "attend1", "out0", "out1", "ln20", "ln21", "up0", "up1",
    "down0", "down1",
)
BACKWARD_ORDER = (
    "down_term", "grad_up0", "up_term", "grad_norm20", "ln2_back0", "out_term", "grad_att0", "attend_back0", "qkv_term", "grad_norm10", "ln1_back0", "time_term",
)


SMALLS = ("g1", "b1", "g2", "b2", "eb")


def bring(sources, targets, sems):
    copies = [pltpu.make_async_copy(a, b, sems.at[i]) for i, (a, b) in enumerate(zip(sources, targets))]
    for copy in copies:
        copy.start()
    return copies


def run_tasks(order, tasks):
    for name in order:
        tasks[name]()


def time_shift(features, weight, pick_seq):
    return nn(jnp.concatenate([pick_seq, pick_seq], axis=1), jnp.concatenate(hi_lo(nn(features, weight)), axis=0))


def first_layer(
    counts_ref, embed_hbm, g1_hbm, b1_hbm, g2_hbm, b2_hbm, eb_hbm,
    wt_hbm, wq_hbm, wo_hbm, we_hbm, wc_hbm,
    feat_ref, bias, xs, *rest
):
    count = len(KEPT)
    kept_hbm, rest = rest[:count], rest[count:]
    weight = SimpleNamespace(**dict(zip("tqoec", rest[:5])))
    kept_refs, rest = rest[5 : 5 + count], rest[5 + count :]
    kept = SimpleNamespace(**dict(zip(KEPT, kept_refs)))
    embed_ref, *smalls = rest[:6]
    later = rest[6]
    mid, in_sem, out_sem, small_sem = rest[7:]
    width = xs.shape[1]
    vocab = embed_ref.shape[0]
    small = SimpleNamespace(**dict(zip(SMALLS, smalls)))
    brought = bring((embed_hbm, g1_hbm, b1_hbm, g2_hbm, b2_hbm, eb_hbm), (embed_ref, *smalls), small_sem)
    loads = Loads(2)
    for index, (name, source) in enumerate(zip("tqoec", (wt_hbm, wq_hbm, wo_hbm, we_hbm, wc_hbm))):
        loads.add(name, source.at[0], getattr(weight, name), in_sem.at[index])
    loads.add("later", wt_hbm.at[1], later, in_sem.at[5])
    loads.begin()
    pushed = []

    def push(*names):
        for name in names:
            index = KEPT.index(name)
            pushed.append(pltpu.make_async_copy(kept_refs[index], kept_hbm[index], out_sem.at[index]))
            pushed[-1].start()

    _, _, pick_char, pick_seq = row_choices()
    masks = side_masks()

    shares = counts_ref.shape[0] // CHUNK
    stamp = []
    for group in range(NGROUPS):
        total = jnp.zeros((1, KPAD), F32)
        for member in range(GROUP):
            value = jnp.zeros((1, 2 * KPAD), F32)
            for share in range(shares):
                value = value + counts_ref[(group * GROUP + member) * shares + share]
            total = total + value[:, 0:KPAD]
            stamp.append(value[:, KPAD:])
        same = row_seq(iota((GROWS, GROWS), 1)) == row_seq(iota((GROWS, GROWS), 0))
        counts = jnp.broadcast_to(total[:, 0:GROWS], (GROWS, GROWS)).T
        live = same & (counts > 0.5)
        bias[group] = jnp.where(live, jnp.log(jnp.maximum(counts, 1.0)), MASKED)
    times = jnp.concatenate(stamp, axis=0)
    half = width // 2
    cycles = [
        times * jnp.exp((iota((1, KPAD), 1) + start).astype(F32) * (-math.log(10000.0) / half))
        for start in range(0, half, KPAD)
    ]
    features = jnp.concatenate(
        [jnp.sin(phase) for phase in cycles] + [jnp.cos(phase) for phase in cycles], axis=1
    ).astype(BF)
    feat_ref[...] = features
    for copy in brought:
        copy.wait()
    loads.need("t")
    xs[...] = nn(pick_char[:, 0:vocab], embed_ref[...]) + time_shift(features, weight.t[...], pick_seq)
    tasks = forward_tasks(0, small, weight, kept, xs, xs, mid, bias, masks, loads.need)
    after = {"ln11": ("unit1", "rstd1", "norm1"), "qkv1": ("qkv",), "attend1": ("probs", "att"),
             "ln21": ("unit2", "rstd2", "norm2"), "up1": ("hid", "slp")}
    for name in FORWARD_ORDER:
        tasks[name]()
        push(*after.get(name, ()))
    loads.need("later")
    xs[...] = xs[...] + time_shift(features, later[...], pick_seq)
    for copy in pushed:
        copy.wait()


def other_layers(
    own_ref, feat_ref, bias, x_ref, chars_hbm, g1_hbm, b1_hbm, g2_hbm, b2_hbm, eb_hbm,
    table_hbm, wt_hbm, wq_hbm, wo_hbm, we_hbm, wc_hbm, *rest, scale
):
    count = len(KEPT)
    layers, width = g1_hbm.shape
    kept_hbm, rest = rest[:count], rest[count:]
    act_hbm, *little_hbm = rest[:7]
    outs = dict(zip(("time", "qkv", "out", "up", "down"), rest[7:12]))
    rest = rest[12:]
    weights, kept = [], []
    for layer in range(layers):
        weights.append(SimpleNamespace(**dict(zip("tqoec", rest[:5]))))
        kept.append(SimpleNamespace(**dict(zip(KEPT, rest[5 : 5 + count]))))
        rest = rest[5 + count :]
    names = ("xs", "mid", "acc", "ga", "gproj", "gscore", "gu", "gb", "gff", "end", "act", "table")
    work = SimpleNamespace(**dict(zip(names, rest)))
    rest = rest[len(names) :]
    stages = dict(zip(outs, rest[:5]))
    little, rest = rest[5:11], rest[11:]
    (chars_ref, *smalls), rest = rest[:6], rest[6:]
    in_sem, kept_sem, out_sem, end_sem, small_sem, little_sem = rest
    eg, g1g, b1g, g2g, b2g, ubg = little
    xs, mid = work.xs, work.mid
    small = SimpleNamespace(**dict(zip(SMALLS, smalls)))
    brought = bring((chars_hbm, g1_hbm, b1_hbm, g2_hbm, b2_hbm, eb_hbm), (chars_ref, *smalls), small_sem)
    grads = SimpleNamespace(eg=eg, g1=g1g, b1=b1g, g2=g2g, b2=b2g, ub=ubg)
    sources = dict(zip("tqoec", (wt_hbm, wq_hbm, wo_hbm, we_hbm, wc_hbm)))
    loads = Loads(DEPTH)
    for layer in range(1, layers):
        for index, name in enumerate("tqoec"):
            if layer == 1 and name == "t":
                continue
            loads.add((layer, name), sources[name].at[layer], getattr(weights[layer], name), in_sem.at[index, layer])
    for name in ("slp", "c", "hid", "e", "norm2", "unit2", "rstd2", "o", "att", "probs", "qkv", "q", "norm1", "unit1", "rstd1"):
        if name in KEPT:
            index = KEPT.index(name)
            loads.add((0, name), kept_hbm[index], getattr(kept[0], name), kept_sem.at[index])
        else:
            loads.add((0, name), sources[name].at[0], getattr(weights[0], name), in_sem.at["tqoec".index(name), 0])
    loads.begin()
    table_copy = pltpu.make_async_copy(table_hbm, work.table, end_sem.at[2])
    table_copy.start()
    queued = {key for key, _ in loads.queue}

    def needs(layer):
        return lambda *names: loads.need(*((layer, name) for name in names if (layer, name) in queued))

    seq_of, char_of, pick_char, pick_seq = row_choices()
    masks = side_masks()
    features = feat_ref[...]
    for copy in brought:
        copy.wait()
    for layer in range(1, layers):
        source = x_ref if layer == 1 else xs
        if layer > 1:
            needs(layer)("t")
            xs[...] = xs[...] + time_shift(features, weights[layer].t[...], pick_seq)
        run_tasks(
            FORWARD_ORDER,
            forward_tasks(layer, small, weights[layer], kept[layer], source, xs, mid, bias, masks, needs(layer)),
        )

    own = own_ref[0]
    work.end[0:NROWS, :] = xs[...].astype(BF)
    work.end[NROWS:, :] = jnp.zeros((work.end.shape[0] - NROWS, width), BF)
    place = chars_ref[...] + lax.rem(own, GROUP) * ROWS
    hot = (place == iota((KPAD, chars_ref.shape[1]), 0)).astype(F32).astype(BF)
    start = pl.multiple_of(lax.div(own, GROUP) * GROWS, 16)
    work.act[...] = tn(hot, work.end[pl.ds(start, KPAD), :]).astype(BF)
    act_copy = pltpu.make_async_copy(work.act, act_hbm, end_sem.at[1])
    act_copy.start()

    slot_row = seq_of * SLOT + char_of
    spread = (slot_row == iota((NROWS, CHUNK * SLOT), 1)).astype(F32).astype(BF)
    table_copy.wait()
    incoming = nn(spread, work.table[...].reshape(CHUNK * SLOT, width)) * scale
    xs[...] = incoming
    work.gff[...] = incoming.astype(BF)

    sends = {}

    def send(name, layer, value):
        if name in sends:
            sends.pop(name).wait()
        stages[name][...] = value()
        copy = pltpu.make_async_copy(
            stages[name], outs[name].at[layer], out_sem.at[list(outs).index(name), layer]
        )
        copy.start()
        sends[name] = copy

    for layer in reversed(range(layers)):
        run_tasks(
            BACKWARD_ORDER,
            backward_tasks(layer, small, weights[layer], kept[layer], work, masks, needs(layer), send,
                           features, (pick_char, pick_seq), grads),
        )
    finals = bring(little, little_hbm, little_sem)
    act_copy.wait()
    for copy in [*sends.values(), *finals]:
        copy.wait()


def vmem():
    return pl.BlockSpec(memory_space=pltpu.VMEM)


def smem():
    return pl.BlockSpec(memory_space=pltpu.SMEM)


def anywhere():
    return pl.BlockSpec(memory_space=pl.ANY)


def call(body, outs, ins, in_specs, out_specs, scratch=(), name=None, mib=8):
    return pl.pallas_call(
        body,
        out_shape=outs,
        in_specs=in_specs,
        out_specs=out_specs,
        scratch_shapes=list(scratch),
        compiler_params=pltpu.CompilerParams(vmem_limit_bytes=mib * MIB),
        name=name,
    )(*ins)


def far(array):
    return pltpu.with_memory_space_constraint(array, pltpu.HBM)


def keep(array):
    return pltpu.with_memory_space_constraint(array, pltpu.VMEM)


def run_forward(counts, weights, big):
    (embed, ln1_gain, ln1_bias, _, _, _, ln2_gain, ln2_bias, _, expand_bias, _) = weights
    width, inner = embed.shape[1], expand_bias.shape[1]
    shapes = kept_shapes(width, inner)
    table = (NROWS, width)
    smalls = (embed, ln1_gain, ln1_bias, ln2_gain, ln2_bias, expand_bias)
    return call(
        first_layer,
        [
            pltpu.VMEM((CHUNK, width), BF),
            pltpu.VMEM((NGROUPS, GROWS, GROWS), F32),
            pltpu.VMEM(table, F32),
        ]
        + [pltpu.HBM(shape, dtype) for shape, dtype in shapes],
        (counts, *map(far, smalls), *map(far, big)),
        [vmem()] + [anywhere()] * (6 + len(big)),
        [vmem()] * 3 + [anywhere()] * len(shapes),
        [pltpu.VMEM(w.shape[1:], w.dtype) for w in big]
        + [pltpu.VMEM(shape, dtype) for shape, dtype in shapes]
        + [
            pltpu.VMEM(small.shape, BF) for small in smalls
        ]
        + [
            pltpu.VMEM(big[0].shape[1:], BF),
            pltpu.VMEM(table, F32),
            pltpu.SemaphoreType.DMA((len(big) + 1,)),
            pltpu.SemaphoreType.DMA((len(shapes),)),
            pltpu.SemaphoreType.DMA((len(smalls),)),
        ],
        name="forward",
        mib=40,
    )


def run_backward(own, chars_row, table, weights, big, passed, scale):
    (embed, ln1_gain, ln1_bias, w_time, w_qkv, w_out, ln2_gain, ln2_bias, expand_weight, expand_bias,
     contract_weight) = weights
    layers, width = ln1_gain.shape
    inner = expand_bias.shape[1]
    shapes = kept_shapes(width, inner)
    positions = chars_row.shape[1]
    whole = (NROWS, width)

    def f32_like(array):
        return jax.ShapeDtypeStruct(array.shape, F32)

    features, bias, x, *kept = passed
    layer_scratch = [pltpu.VMEM(w.shape[1:], w.dtype) for w in big] + [
        pltpu.VMEM(shape, dtype) for shape, dtype in shapes
    ]
    smalls = (ln1_gain, ln1_bias, ln2_gain, ln2_bias, expand_bias)
    little = (embed, *smalls)
    outs = call(
        lambda *refs: other_layers(*refs, scale=scale),
        [jax.ShapeDtypeStruct((positions, width), BF)]
        + [f32_like(w) for w in (*little, w_time, w_qkv, w_out, expand_weight, contract_weight)],
        (own, keep(features), keep(bias), keep(x), far(chars_row), *map(far, smalls), keep(table), *map(far, big),
         *map(far, kept)),
        [smem()] + [vmem()] * 3 + [anywhere()] * (7 + len(big) + len(kept)),
        [anywhere()] * 12,
        layer_scratch * layers
        + [
            pltpu.VMEM(whole, F32),
            pltpu.VMEM(whole, F32),
            pltpu.VMEM(whole, F32),
            pltpu.VMEM(whole, BF),
            pltpu.VMEM((NROWS, 3 * width), BF),
            pltpu.VMEM((HEADS // 2, 2 * GROWS, GROWS), BF),
            pltpu.VMEM((NROWS, inner), BF),
            pltpu.VMEM(whole, BF),
            pltpu.VMEM(whole, BF),
            pltpu.VMEM((NROWS + KPAD - GROWS, width), BF),
            pltpu.VMEM((positions, width), BF),
            pltpu.VMEM(table.shape, BF),
        ]
        + [pltpu.VMEM(w.shape[1:], F32) for w in big]
        + [pltpu.VMEM(w.shape, F32) for w in little]
        + [pltpu.VMEM(chars_row.shape, I32)]
        + [pltpu.VMEM(small.shape, BF) for small in smalls]
        + [
            pltpu.SemaphoreType.DMA((len(big), layers)),
            pltpu.SemaphoreType.DMA((len(shapes),)),
            pltpu.SemaphoreType.DMA((len(big), layers)),
            pltpu.SemaphoreType.DMA((3,)),
            pltpu.SemaphoreType.DMA((1 + len(smalls),)),
            pltpu.SemaphoreType.DMA((len(little),)),
        ],
        name="backward",
        mib=60,
    )
    act, eg, g1, b1, g2, b2, ub, tg, qg, og, ug, dg = outs
    return act, (eg, g1, b1, tg, qg, og, g2, b2, ug, ub, dg)


def per_device(chars, timesteps, *rest):
    weights, cotangent = rest[:-1], rest[-1]
    width = weights[0].shape[1]
    n_dp, n_blk = lax.axis_size("dp"), lax.axis_size("blk")
    seq = lax.axis_index("dp")
    positions = chars.shape[0]
    chars_row = chars.reshape(1, positions)
    big = [weights[i] for i in (3, 4, 5, 8, 10)]
    counts, sums = call(
        lambda *refs: local_sums(*refs, shares=n_blk),
        [
            jax.ShapeDtypeStruct((n_dp * n_blk, 1, 2 * KPAD), F32),
            jax.ShapeDtypeStruct((SLOT, width), F32),
        ],
        (
            far(chars_row),
            far(cotangent.reshape(positions, width)),
            (seq % GROUP).astype(I32).reshape(1),
            timesteps,
        ),
        [vmem(), vmem(), smem(), smem()],
        [vmem(), vmem()],
        name="local_sums",
    )
    counts = lax.all_to_all(counts, ("dp", "blk"), split_axis=0, concat_axis=0, tiled=True)
    parts = [sums] + [
        lax.ppermute(sums, "blk", [(i, (i + step) % n_blk) for i in range(n_blk)])
        for step in range(1, n_blk)
    ]
    table = call(
        spread_sums,
        jax.ShapeDtypeStruct((n_dp, SLOT, width), BF),
        parts,
        [vmem()] * len(parts),
        vmem(),
        name="spread_sums",
    )
    table = lax.all_to_all(table, "dp", split_axis=0, concat_axis=0, tiled=True)
    scale = 1.0 / (n_dp * n_blk)
    if n_dp == CHUNK:
        kept = run_forward(counts, weights, big)
        act, grads = run_backward(seq.reshape(1).astype(I32), chars_row, table, weights, big, kept, scale)
    else:

        def step(carry, chunk):
            act, grads = carry
            place = seq - chunk * CHUNK
            inside = (place >= 0) & (place < CHUNK)
            here = lax.dynamic_slice_in_dim(counts, chunk * CHUNK * n_blk, CHUNK * n_blk, axis=0)
            part = lax.dynamic_slice_in_dim(table, chunk * CHUNK, CHUNK, axis=0)
            own = jnp.clip(place, 0, CHUNK - 1).reshape(1).astype(I32)
            kept = run_forward(here, weights, big)
            new_act, new_grads = run_backward(own, chars_row, part, weights, big, kept, scale)
            return (jnp.where(inside, new_act, act), tuple(a + b for a, b in zip(grads, new_grads))), None

        start = (jnp.zeros((positions, width), BF), tuple(jnp.zeros(w.shape, F32) for w in weights))
        (act, grads), _ = lax.scan(step, start, jnp.arange(n_dp // CHUNK, dtype=I32))
    return (act.reshape(positions, 1, width), *grads)


def solution(mesh):
    in_specs = (P("blk", "dp"), P("dp")) + (P(),) * 11 + (P("blk", "dp", None),)
    out_specs = (P("blk", "dp", None),) + (P(),) * 11
    return jax.shard_map(
        per_device, mesh=mesh, in_specs=in_specs, out_specs=out_specs, check_vma=False
    )
```

```python
import math
from types import SimpleNamespace

import jax
import jax.numpy as jnp
from jax import lax
from jax.experimental import pallas as pl
from jax.experimental.pallas import tpu as pltpu
from jax.sharding import PartitionSpec as P

HEADS = 8
HEAD = 64
ROWS = 28
GROUP = 4
GROWS = ROWS * GROUP
CHUNK = 16
NROWS = ROWS * CHUNK
NGROUPS = CHUNK // GROUP
KPAD = 128
SLOT = 32
PIECE = 512
HALF = NROWS // 2
MASKED = -1e30
BF = jnp.bfloat16
F32 = jnp.float32
I32 = jnp.int32
MIB = 2**20
DEPTH = 2
GSTRIP = 112
NSTRIP = 112
WIDE = 256
BAND = 512
PER_TASK = 1


def nn(a, b):
    return lax.dot_general(a, b, (((1,), (0,)), ((), ())), preferred_element_type=F32)


def nt(a, b):
    return lax.dot_general(a, b, (((1,), (1,)), ((), ())), preferred_element_type=F32)


def tn(a, b):
    return lax.dot_general(a, b, (((0,), (0,)), ((), ())), preferred_element_type=F32)


def iota(shape, dim):
    return lax.broadcasted_iota(I32, shape, dim)


def hi_lo(values):
    high = values.astype(BF)
    return high, (values - high.astype(F32)).astype(BF)


def row_seq(index):
    return lax.shift_right_logical(index * (65536 // ROWS + 1), 16)


def local_sums(chars_ref, cot_ref, place_ref, time_ref, count_ref, sum_ref, *, shares):
    positions = chars_ref.shape[1]
    chars = chars_ref[...]
    placed = (chars + place_ref[0] * ROWS == iota((KPAD, positions), 0)).astype(F32)
    counts = nt(jnp.ones((8, positions), BF), placed.astype(BF))[0:1]
    stamp = jnp.full((1, KPAD), time_ref[0].astype(F32) * (1.0 / shares), F32)
    row = jnp.concatenate([counts, stamp], axis=1)
    for device in range(count_ref.shape[0]):
        count_ref[device] = row
    onehot = (chars == iota((SLOT, positions), 0)).astype(F32)
    sum_ref[...] = nn(onehot.astype(BF), cot_ref[...])


def spread_sums(*refs):
    total = refs[0][...]
    for ref in refs[1:-1]:
        total = total + ref[...]
    total = total.astype(BF)
    for device in range(refs[-1].shape[0]):
        refs[-1][device] = total


class Loads:
    def __init__(self, depth):
        self.depth, self.queue, self.done = depth, [], set()

    def add(self, key, source, target, sem):
        self.queue.append((key, pltpu.make_async_copy(source, target, sem)))

    def begin(self):
        self.started = 0
        self.advance(self.depth)

    def need(self, *keys):
        for key in keys:
            while key not in self.done:
                if len(self.done) == self.started:
                    self.advance(1)
                first, copy = self.queue[len(self.done)]
                copy.wait()
                self.done.add(first)

    def advance(self, count):
        for _, copy in self.queue[self.started : self.started + count]:
            copy.start()
        self.started = min(self.started + count, len(self.queue))


def normalise(values):
    mean = jnp.mean(values, axis=-1, keepdims=True)
    centered = values - mean
    rstd = lax.rsqrt(jnp.mean(centered * centered, axis=-1, keepdims=True) + 1e-05)
    return centered * rstd, rstd


def norm_back(grad_out, unit, rstd, gain):
    scaled = grad_out * gain
    return rstd * (
        scaled
        - jnp.mean(scaled, axis=-1, keepdims=True)
        - unit * jnp.mean(scaled * unit, axis=-1, keepdims=True)
    )


def gelu_and_slope(up):
    size = jnp.abs(up)
    bell = jnp.exp2((-0.5 / math.log(2.0)) * (up * up))
    shift = math.sqrt(2.0) / 0.3275911
    ratio = 1.0 / (shift + size)
    poly = 0.5 * shift**5 * 1.061405429
    for power, term in ((4, -1.453152027), (3, 1.421413741), (2, -0.284496736), (1, 0.254829592)):
        poly = poly * ratio + 0.5 * shift**power * term
    tail = (poly * ratio) * bell
    slope = tail - (size * bell) * (1.0 / math.sqrt(2 * math.pi))
    return jnp.maximum(up, 0.0) - size * tail, jnp.where(up > 0, 1.0 - slope, slope)


def row_choices():
    row = iota((NROWS, 1), 0)
    seq_of = row_seq(row)
    char_of = row - seq_of * ROWS
    pick_char = (char_of == iota((NROWS, SLOT), 1)).astype(F32).astype(BF)
    pick_seq = (seq_of == iota((NROWS, CHUNK), 1)).astype(F32).astype(BF)
    return seq_of, char_of, pick_char, pick_seq


def side_masks():
    left = (iota((GROWS, KPAD), 1) < HEAD).astype(F32)
    return left.astype(BF), (1.0 - left).astype(BF)


def blocks(qkv, masks, group, pair, part):
    lanes = part * (qkv.shape[1] // 3) + pair * KPAD
    both = qkv[group * GROWS : (group + 1) * GROWS, lanes : lanes + KPAD]
    return jnp.concatenate([both * masks[0], both * masks[1]], axis=0)


def wide(ref, layer):
    return ref[layer : layer + 1, :].astype(F32)


EARLY = ("unit1", "rstd1", "norm1", "qkv", "probs")
KEPT = ("unit1", "rstd1", "norm1", "qkv", "probs", "att", "unit2", "rstd2", "norm2", "hid", "slp")


def kept_shapes(width, inner):
    row = {"rstd1": (KPAD, F32), "rstd2": (KPAD, F32), "qkv": (3 * width, BF), "hid": (inner, BF), "slp": (inner, BF)}
    shapes = {name: ((NROWS, row.get(name, (width, BF))[0]), row.get(name, (width, BF))[1]) for name in KEPT}
    shapes["probs"] = ((NGROUPS, HEADS // 2, 2 * GROWS, GROWS), BF)
    return [shapes[name] for name in KEPT]


def halves(size=HALF):
    return [slice(start, start + size) for start in range(0, NROWS, size)]


def strips(span, rows):
    return [slice(start, start + rows) for start in range(span.start, span.stop, rows)]


def groups_of(span):
    return range(span.start // GROWS, span.stop // GROWS)


def forward_tasks(layer, small, weight, kept, source, xs, mid, bias, masks, need, brought, shifted=None):
    width = xs.shape[1]
    inner = kept.hid.shape[1]
    pairs = width // KPAD

    def normed(span, values, unit_ref, rstd_ref, norm_ref, gain, shift):
        unit, rstd = normalise(values[span, :])
        while brought:
            brought.pop().wait()
        unit_ref[span, :] = unit.astype(BF)
        rstd_ref[span, :] = jnp.broadcast_to(rstd, (rstd.shape[0], KPAD))
        norm_ref[span, :] = (unit * wide(gain, layer) + wide(shift, layer)).astype(BF)

    def ln1(span):
        normed(span, source, kept.unit1, kept.rstd1, kept.norm1, small.g1, small.b1)

    def qkv(span):
        need("q")
        for part in range(3):
            lanes = slice(part * width, (part + 1) * width)
            product = nn(kept.norm1[span, :], weight.q[:, lanes])
            kept.qkv[span, lanes] = (product * 0.125 if part == 0 else product).astype(BF)

    def attend(span):
        for group in groups_of(span):
            rows = slice(group * GROWS, (group + 1) * GROWS)
            lanes = [slice(pair * KPAD, (pair + 1) * KPAD) for pair in range(pairs)]
            scores = [
                nt(blocks(kept.qkv, masks, group, pair, 1), kept.qkv[rows, lanes[pair]]) for pair in range(pairs)
            ]
            yield
            for pair in range(pairs):
                for side in range(2):
                    keys = slice(side * GROWS, (side + 1) * GROWS)
                    score = scores[pair][keys] + bias[group]
                    heft = jnp.exp(score - jnp.max(score, axis=0, keepdims=True))
                    prob = heft * (1.0 / jnp.sum(heft, axis=0, keepdims=True))
                    kept.probs[group, pair, keys, :] = prob.astype(BF)
            yield
            for pair in range(pairs):
                kept.att[rows, lanes[pair]] = tn(
                    kept.probs[group, pair], blocks(kept.qkv, masks, group, pair, 2)
                ).astype(BF)
            yield

    def out(span):
        need("o")
        mid[span, :] = source[span, :] + nn(kept.att[span, :], weight.o[...])

    def ln2(span):
        normed(span, mid, kept.unit2, kept.rstd2, kept.norm2, small.g2, small.b2)

    def up(span):
        need("e")
        for piece in range(inner // PIECE):
            cols = slice(piece * PIECE, (piece + 1) * PIECE)
            product = nn(kept.norm2[span, :], weight.e[:, cols])
            shift = small.eb[layer : layer + 1, cols].astype(F32)
            for rows in strips(span, GSTRIP):
                strip = product[rows.start - span.start : rows.stop - span.start]
                hidden, slope = gelu_and_slope(strip + shift)
                kept.hid[rows, cols] = hidden.astype(BF)
                kept.slp[rows, cols] = slope.astype(BF)
                yield

    def down(span):
        need("c")
        for start in range(0, width, WIDE):
            cols = slice(start, start + WIDE)
            total = mid[span, cols] + nn(kept.hid[span, :], weight.c[:, cols])
            xs[span, cols] = total if shifted is None else total + shifted[span, cols]
            yield

    parts = dict(ln1=ln1, qkv=qkv, attend=attend, out=out, ln2=ln2, up=up, down=down)
    return {
        f"{name}{half}": (lambda part=part, span=span: part(span))
        for name, part in parts.items()
        for half, span in enumerate(halves())
    }


def backward_tasks(layer, small, weight, kept, work, masks, need, send, features, picks, grads):
    xs, mid, acc = work.xs, work.mid, work.acc
    width = xs.shape[1]
    inner = kept.hid.shape[1]
    pairs = width // KPAD
    left_lanes = iota((GROWS, KPAD), 1) < HEAD

    def add_rows(ref, span, value, cols=slice(None)):
        total = jnp.sum(value, axis=0, keepdims=True)
        ref[layer : layer + 1, cols] = total if span.start == 0 else ref[layer : layer + 1, cols] + total

    def grad_up(span):
        need("c", "slp")
        for piece in range(inner // PIECE):
            cols = slice(piece * PIECE, (piece + 1) * PIECE)
            value = nt(work.gff[span, :], weight.c[cols, :]) * kept.slp[span, cols].astype(F32)
            add_rows(grads.ub, span, value, cols)
            work.gu[span, cols] = value.astype(BF)

    def grad_norm2(span):
        need("e")
        acc[span, :] = nt(work.gu[span, :], weight.e[...])

    def ln2_back(span):
        need("unit2", "rstd2")
        for rows in strips(span, NSTRIP):
            unit, grad = kept.unit2[rows, :].astype(F32), acc[rows, :]
            add_rows(grads.g2, rows, grad * unit)
            add_rows(grads.b2, rows, grad)
            total = xs[rows, :] + norm_back(grad, unit, kept.rstd2[rows, 0:1], wide(small.g2, layer))
            mid[rows, :] = total
            work.gb[rows, :] = total.astype(BF)
            yield

    def grad_att(span):
        need("o")
        work.ga[span, :] = nt(work.gb[span, :], weight.o[...]).astype(BF)

    def attend_back(span):
        need("qkv", "probs")
        for group in groups_of(span):
            rows = slice(group * GROWS, (group + 1) * GROWS)
            lanes = [slice(pair * KPAD, (pair + 1) * KPAD) for pair in range(pairs)]
            grad_probs = [
                nt(blocks(kept.qkv, masks, group, pair, 2), work.ga[rows, lanes[pair]]) for pair in range(pairs)
            ]
            yield
            for pair in range(pairs):
                for side in range(2):
                    keys = slice(side * GROWS, (side + 1) * GROWS)
                    prob = kept.probs[group, pair, keys, :].astype(F32)
                    grad_prob = grad_probs[pair][keys]
                    delta = jnp.sum(prob * grad_prob, axis=0, keepdims=True)
                    work.gscore[pair, keys, :] = (prob * (grad_prob - delta)).astype(BF)
            yield
            for pair in range(pairs):
                grad_score = work.gscore[pair]
                work.gproj[rows, lanes[pair]] = (
                    tn(grad_score, blocks(kept.qkv, masks, group, pair, 1)) * 0.125
                ).astype(BF)
                grad_key = nn(grad_score, kept.qkv[rows, lanes[pair]])
                grad_value = nn(kept.probs[group, pair], work.ga[rows, lanes[pair]])
                for part, product in ((1, grad_key), (2, grad_value)):
                    joined = jnp.where(left_lanes, product[0:GROWS], product[GROWS : 2 * GROWS])
                    start = part * width + pair * KPAD
                    work.gproj[rows, start : start + KPAD] = joined.astype(BF)
            yield

    def grad_norm1(span):
        need("q")
        acc[span, :] = nt(work.gproj[span, :], weight.q[...])

    def ln1_back(span):
        need("unit1", "rstd1")
        for rows in strips(span, NSTRIP):
            unit, grad = kept.unit1[rows, :].astype(F32), acc[rows, :]
            add_rows(grads.g1, rows, grad * unit)
            add_rows(grads.b1, rows, grad)
            total = mid[rows, :] + norm_back(grad, unit, kept.rstd1[rows, 0:1], wide(small.g1, layer))
            xs[rows, :] = total
            work.gff[rows, :] = total.astype(BF)
            yield

    def down_term():
        need("hid")
        yield from send("down", layer, kept.hid, work.gff)

    def up_term():
        need("norm2")
        yield from send("up", layer, kept.norm2, work.gu)

    def out_term():
        need("att")
        yield from send("out", layer, kept.att, work.gb)

    def qkv_term():
        need("norm1")
        yield from send("qkv", layer, kept.norm1, work.gproj)

    def time_term():
        pick_char, pick_seq = picks
        by_seq = tn(pick_seq, work.gff[...]).astype(BF)
        yield from send("time", layer, features, by_seq)
        if layer == 0:
            grads.eg[...] = tn(pick_char, work.gff[...])[0 : grads.eg.shape[0]]

    by_half = dict(
        grad_up=grad_up, grad_norm2=grad_norm2, ln2_back=ln2_back, grad_att=grad_att,
        attend_back=attend_back, grad_norm1=grad_norm1, ln1_back=ln1_back,
    )
    tasks = {
        f"{name}{half}": (lambda part=part, span=span: part(span))
        for name, part in by_half.items()
        for half, span in enumerate(halves(NROWS))
    }
    tasks.update(down_term=down_term, up_term=up_term, out_term=out_term, qkv_term=qkv_term, time_term=time_term)
    return tasks


FIRST_ORDER = (
    "ln10", "ln11", "qkv0", "qkv1", "attend0", "attend1", "out0", "out1", "shift0", "ln20", "ln21", "up0", "up1",
    "down0", "down1",
)
SECOND_ORDER = ("ln10", "ln11", "qkv0", "qkv1", "attend0", "attend1")
LATTER_ORDER = ("out0", "out1", "ln20", "ln21", "up0", "down0|up1", "down1")
FORWARD_ORDER = (
    "ln10", "ln11", "qkv0", "qkv1", "attend0", "out0", "ln20", "attend1|up0", "out1", "ln21", "down0|up1", "down1",
)
BACKWARD_ORDER = (
    "down_term", "grad_up0", "up_term", "grad_norm20", "ln2_back0", "out_term", "grad_att0", "attend_back0", "qkv_term", "grad_norm10", "ln1_back0", "time_term",
)


SMALLS = ("g1", "b1", "g2", "b2", "eb")


def bring(sources, targets, sems):
    copies = [pltpu.make_async_copy(a, b, sems.at[i]) for i, (a, b) in enumerate(zip(sources, targets))]
    for copy in copies:
        copy.start()
    return copies


def run_parts(names, tasks):
    steps = [step for step in (tasks[name]() for name in names.split("|")) if step is not None]
    while steps:
        steps = [step for step in steps if next(step, steps) is not steps]


def run_tasks(order, tasks, loads):
    for names in order:
        run_parts(names, tasks)
        loads.advance(PER_TASK)


def time_shift(features, weight, pick_seq):
    return nn(jnp.concatenate([pick_seq, pick_seq], axis=1), jnp.concatenate(hi_lo(nn(features, weight)), axis=0))


def first_layer(
    counts_ref, embed_hbm, g1_hbm, b1_hbm, g2_hbm, b2_hbm, eb_hbm,
    wt_hbm, wq_hbm, wo_hbm, we_hbm, wc_hbm,
    feat_ref, xs, next_att, next_o, *rest
):
    count = len(KEPT)
    kept_hbm, early_hbm, rest = rest[:count], rest[count : count + len(EARLY)], rest[count + len(EARLY) :]
    weight = SimpleNamespace(**dict(zip("tqoec", rest[:5])))
    kept_refs, rest = rest[5 : 5 + count], rest[5 + count :]
    kept = SimpleNamespace(**dict(zip(KEPT, kept_refs)))
    early_refs, rest = rest[: len(EARLY)], rest[len(EARLY) :]
    early = SimpleNamespace(att=next_att, hid=kept.hid, **dict(zip(EARLY, early_refs)))
    embed_ref, *smalls = rest[:6]
    later, next_q, bias, mid, shifted, in_sem, out_sem, early_sem, small_sem = rest[6:]
    width = xs.shape[1]
    vocab = embed_ref.shape[0]
    small = SimpleNamespace(**dict(zip(SMALLS, smalls)))
    brought = bring((embed_hbm, g1_hbm, b1_hbm, g2_hbm, b2_hbm, eb_hbm), (embed_ref, *smalls), small_sem)
    loads = Loads(2)
    for index, (name, source) in enumerate(zip("tqoec", (wt_hbm, wq_hbm, wo_hbm, we_hbm, wc_hbm))):
        loads.add(name, source.at[0], getattr(weight, name), in_sem.at[index])
        if name == "o":
            loads.add("later", wt_hbm.at[1], later, in_sem.at[5])
    loads.add("next_q", wq_hbm.at[1], next_q, in_sem.at[6])
    loads.add("next_o", wo_hbm.at[1], next_o, in_sem.at[7])
    loads.begin()
    pushed = []

    def push(half, names, sources, targets, sems, wanted):
        for name in wanted:
            index = names.index(name)
            unit = GROWS if name == "probs" else 1
            rows = pl.ds(half * HALF // unit, HALF // unit)
            pushed.append(
                pltpu.make_async_copy(sources[index].at[rows], targets[index].at[rows], sems.at[index, half])
            )
            pushed[-1].start()

    _, _, pick_char, pick_seq = row_choices()
    masks = side_masks()

    shares = counts_ref.shape[0] // CHUNK
    stamp = []
    for group in range(NGROUPS):
        total = jnp.zeros((1, KPAD), F32)
        for member in range(GROUP):
            value = jnp.zeros((1, 2 * KPAD), F32)
            for share in range(shares):
                value = value + counts_ref[(group * GROUP + member) * shares + share]
            total = total + value[:, 0:KPAD]
            stamp.append(value[:, KPAD:])
        same = row_seq(iota((GROWS, GROWS), 1)) == row_seq(iota((GROWS, GROWS), 0))
        counts = jnp.broadcast_to(total[:, 0:GROWS], (GROWS, GROWS)).T
        live = same & (counts > 0.5)
        bias[group] = jnp.where(live, jnp.log(jnp.maximum(counts, 1.0)), MASKED)
    times = jnp.concatenate(stamp, axis=0)
    half = width // 2
    cycles = [
        times * jnp.exp((iota((1, KPAD), 1) + start).astype(F32) * (-math.log(10000.0) / half))
        for start in range(0, half, KPAD)
    ]
    features = jnp.concatenate(
        [jnp.sin(phase) for phase in cycles] + [jnp.cos(phase) for phase in cycles], axis=1
    ).astype(BF)
    feat_ref[...] = features
    while brought:
        brought.pop().wait()
    loads.need("t")
    xs[...] = nn(pick_char[:, 0:vocab], embed_ref[...]) + time_shift(features, weight.t[...], pick_seq)
    tasks = forward_tasks(0, small, weight, kept, xs, xs, mid, bias, masks, loads.need, brought, shifted)

    def shift_next():
        loads.need("later")
        shifted[...] = time_shift(features, later[...], pick_seq)

    tasks["shift0"] = shift_next
    after = {"ln1": ("unit1", "rstd1", "norm1"), "qkv": ("qkv",), "attend": ("probs", "att"),
             "ln2": ("unit2", "rstd2", "norm2"), "up": ("hid", "slp")}
    second = forward_tasks(
        1, small, SimpleNamespace(q=next_q, o=next_o), early, xs, xs, mid, bias, masks,
        lambda name: loads.need("next_" + name), brought,
    )
    for order, work, target in (
        (FIRST_ORDER, tasks, (KEPT, kept_refs, kept_hbm, out_sem)),
        (SECOND_ORDER, second, (EARLY, early_refs, early_hbm, early_sem)),
    ):
        for names in order:
            run_parts(names, work)
            loads.advance(PER_TASK)
            for name in names.split("|"):
                wanted = [array for array in after.get(name[:-1], ()) if array in target[0]]
                push(int(name[-1]), *target, wanted)
    loads.need("next_o")
    for copy in pushed:
        copy.wait()


def other_layers(
    own_ref, feat_ref, x_ref, att_ref, o_ref, chars_hbm, g1_hbm, b1_hbm, g2_hbm, b2_hbm, eb_hbm,
    table_hbm, wt_hbm, wq_hbm, wo_hbm, we_hbm, wc_hbm, *rest, scale
):
    count = len(KEPT)
    layers, width = g1_hbm.shape
    kept_hbm, early_hbm, rest = rest[:count], rest[count : count + len(EARLY)], rest[count + len(EARLY) :]
    act_hbm, *little_hbm = rest[:7]
    outs = dict(zip(("time", "qkv", "out", "up", "down"), rest[7:12]))
    rest = rest[12:]
    weights, kept = [], []
    for layer in range(layers):
        weights.append(SimpleNamespace(**dict(zip("tqoec", rest[:5]))))
        kept.append(SimpleNamespace(**dict(zip(KEPT, rest[5 : 5 + count]))))
        rest = rest[5 + count :]
    weights[1].o, kept[1].att = o_ref, att_ref
    names = ("xs", "mid", "acc", "ga", "gproj", "gscore", "gu", "gb", "gff", "end", "act", "table")
    work = SimpleNamespace(**dict(zip(names, rest)))
    rest = rest[len(names) :]
    stages = dict(zip(outs, rest[:5]))
    little, rest = rest[5:11], rest[11:]
    (chars_ref, *smalls), rest = rest[:6], rest[6:]
    in_sem, kept_sem, early_sem, out_sem, end_sem, small_sem, little_sem = rest
    eg, g1g, b1g, g2g, b2g, ubg = little
    xs, mid = work.xs, work.mid
    small = SimpleNamespace(**dict(zip(SMALLS, smalls)))
    brought = bring((chars_hbm, g1_hbm, b1_hbm, g2_hbm, b2_hbm, eb_hbm), (chars_ref, *smalls), small_sem)
    grads = SimpleNamespace(eg=eg, g1=g1g, b1=b1g, g2=g2g, b2=b2g, ub=ubg)
    sources = dict(zip("tqoec", (wt_hbm, wq_hbm, wo_hbm, we_hbm, wc_hbm)))
    loads = Loads(DEPTH)
    for layer in range(1, layers):
        for name in "ec" if layer == 1 else "tqoec":
            loads.add(
                (layer, name), sources[name].at[layer], getattr(weights[layer], name), in_sem.at["tqoec".index(name), layer]
            )
    for name in ("probs", "qkv", "norm1", "q", "unit1", "rstd1"):
        if name in EARLY:
            index = EARLY.index(name)
            loads.add((1, name), early_hbm[index], getattr(kept[1], name), early_sem.at[index])
        else:
            loads.add((1, name), sources[name].at[1], weights[1].q, in_sem.at["tqoec".index(name), 1])
    for name in ("slp", "c", "hid", "e", "norm2", "unit2", "rstd2", "o", "att", "probs", "qkv", "q", "norm1", "unit1", "rstd1"):
        if name in KEPT:
            index = KEPT.index(name)
            loads.add((0, name), kept_hbm[index], getattr(kept[0], name), kept_sem.at[index])
        else:
            loads.add((0, name), sources[name].at[0], getattr(weights[0], name), in_sem.at["tqoec".index(name), 0])
    loads.begin()
    table_copy = pltpu.make_async_copy(table_hbm, work.table, end_sem.at[2])
    table_copy.start()
    queued = {key for key, _ in loads.queue}

    def needs(layer):
        return lambda *names: loads.need(*((layer, name) for name in names if (layer, name) in queued))

    seq_of, char_of, pick_char, pick_seq = row_choices()
    masks = side_masks()
    features = feat_ref[...]
    for layer in range(1, layers):
        source, order = (x_ref, LATTER_ORDER) if layer == 1 else (xs, FORWARD_ORDER)
        if layer > 1:
            needs(layer)("t")
            xs[...] = xs[...] + time_shift(features, weights[layer].t[...], pick_seq)
        run_tasks(
            order,
            forward_tasks(layer, small, weights[layer], kept[layer], source, xs, mid, None, masks, needs(layer), brought),
            loads,
        )

    own = own_ref[0]
    work.end[0:NROWS, :] = xs[...].astype(BF)
    work.end[NROWS:, :] = jnp.zeros((work.end.shape[0] - NROWS, width), BF)
    place = chars_ref[...] + lax.rem(own, GROUP) * ROWS
    hot = (place == iota((KPAD, chars_ref.shape[1]), 0)).astype(F32).astype(BF)
    start = pl.multiple_of(lax.div(own, GROUP) * GROWS, 16)
    work.act[...] = tn(hot, work.end[pl.ds(start, KPAD), :]).astype(BF)
    act_copy = pltpu.make_async_copy(work.act, act_hbm, end_sem.at[1])
    act_copy.start()

    slot_row = seq_of * SLOT + char_of
    spread = (slot_row == iota((NROWS, CHUNK * SLOT), 1)).astype(F32).astype(BF)
    table_copy.wait()
    incoming = nn(spread, work.table[...].reshape(CHUNK * SLOT, width)) * scale
    xs[...] = incoming
    work.gff[...] = incoming.astype(BF)

    sends = {}

    def send(name, layer, left, right):
        if name in sends:
            sends.pop(name).wait()
        stage = stages[name]
        for start in range(0, stage.shape[0], BAND):
            stage[start : start + BAND, :] = tn(left[:, start : start + BAND], right[...])
            yield
        copy = pltpu.make_async_copy(stage, outs[name].at[layer], out_sem.at[list(outs).index(name), layer])
        copy.start()
        sends[name] = copy

    for layer in reversed(range(layers)):
        run_tasks(
            BACKWARD_ORDER,
            backward_tasks(layer, small, weights[layer], kept[layer], work, masks, needs(layer), send,
                           features, (pick_char, pick_seq), grads),
            loads,
        )
    finals = bring(little, little_hbm, little_sem)
    act_copy.wait()
    for copy in [*sends.values(), *finals]:
        copy.wait()


def vmem():
    return pl.BlockSpec(memory_space=pltpu.VMEM)


def smem():
    return pl.BlockSpec(memory_space=pltpu.SMEM)


def anywhere():
    return pl.BlockSpec(memory_space=pl.ANY)


def call(body, outs, ins, in_specs, out_specs, scratch=(), name=None, mib=8):
    return pl.pallas_call(
        body,
        out_shape=outs,
        in_specs=in_specs,
        out_specs=out_specs,
        scratch_shapes=list(scratch),
        compiler_params=pltpu.CompilerParams(vmem_limit_bytes=mib * MIB),
        name=name,
    )(*ins)


def far(array):
    return pltpu.with_memory_space_constraint(array, pltpu.HBM)


def keep(array):
    return pltpu.with_memory_space_constraint(array, pltpu.VMEM)


def run_forward(counts, weights, big):
    (embed, ln1_gain, ln1_bias, _, _, _, ln2_gain, ln2_bias, _, expand_bias, _) = weights
    width, inner = embed.shape[1], expand_bias.shape[1]
    shapes = kept_shapes(width, inner)
    early = [shapes[KEPT.index(name)] for name in EARLY]
    table = (NROWS, width)
    smalls = (embed, ln1_gain, ln1_bias, ln2_gain, ln2_bias, expand_bias)
    return call(
        first_layer,
        [
            pltpu.VMEM((CHUNK, width), BF),
            pltpu.VMEM(table, F32),
            pltpu.VMEM(table, BF),
            pltpu.VMEM(big[2].shape[1:], BF),
        ]
        + [pltpu.HBM(shape, dtype) for shape, dtype in shapes + early],
        (counts, *map(far, smalls), *map(far, big)),
        [vmem()] + [anywhere()] * (6 + len(big)),
        [vmem()] * 4 + [anywhere()] * (len(shapes) + len(early)),
        [pltpu.VMEM(w.shape[1:], w.dtype) for w in big]
        + [pltpu.VMEM(shape, dtype) for shape, dtype in shapes + early]
        + [pltpu.VMEM(small.shape, BF) for small in smalls]
        + [
            pltpu.VMEM(big[0].shape[1:], BF),
            pltpu.VMEM(big[1].shape[1:], BF),
            pltpu.VMEM((NGROUPS, GROWS, GROWS), F32),
            pltpu.VMEM(table, F32),
            pltpu.VMEM(table, F32),
            pltpu.SemaphoreType.DMA((len(big) + 3,)),
            pltpu.SemaphoreType.DMA((len(shapes), NROWS // HALF)),
            pltpu.SemaphoreType.DMA((len(early), NROWS // HALF)),
            pltpu.SemaphoreType.DMA((len(smalls),)),
        ],
        name="forward",
        mib=40,
    )


def run_backward(own, chars_row, table, weights, big, passed, scale):
    (embed, ln1_gain, ln1_bias, w_time, w_qkv, w_out, ln2_gain, ln2_bias, expand_weight, expand_bias,
     contract_weight) = weights
    layers, width = ln1_gain.shape
    inner = expand_bias.shape[1]
    shapes = kept_shapes(width, inner)
    positions = chars_row.shape[1]
    whole = (NROWS, width)

    def f32_like(array):
        return jax.ShapeDtypeStruct(array.shape, F32)

    features, x, att, next_o, *kept = passed
    layer_scratch = [pltpu.VMEM(w.shape[1:], w.dtype) for w in big] + [
        pltpu.VMEM(shape, dtype) for shape, dtype in shapes
    ]
    smalls = (ln1_gain, ln1_bias, ln2_gain, ln2_bias, expand_bias)
    little = (embed, *smalls)
    outs = call(
        lambda *refs: other_layers(*refs, scale=scale),
        [jax.ShapeDtypeStruct((positions, width), BF)]
        + [f32_like(w) for w in (*little, w_time, w_qkv, w_out, expand_weight, contract_weight)],
        (own, keep(features), keep(x), keep(att), keep(next_o), far(chars_row), *map(far, smalls), keep(table), *map(far, big),
         *map(far, kept)),
        [smem()] + [vmem()] * 4 + [anywhere()] * (7 + len(big) + len(kept)),
        [anywhere()] * 12,
        layer_scratch * layers
        + [
            pltpu.VMEM(whole, F32),
            pltpu.VMEM(whole, F32),
            pltpu.VMEM(whole, F32),
            pltpu.VMEM(whole, BF),
            pltpu.VMEM((NROWS, 3 * width), BF),
            pltpu.VMEM((HEADS // 2, 2 * GROWS, GROWS), BF),
            pltpu.VMEM((NROWS, inner), BF),
            pltpu.VMEM(whole, BF),
            pltpu.VMEM(whole, BF),
            pltpu.VMEM((NROWS + KPAD - GROWS, width), BF),
            pltpu.VMEM((positions, width), BF),
            pltpu.VMEM(table.shape, BF),
        ]
        + [pltpu.VMEM(w.shape[1:], F32) for w in big]
        + [pltpu.VMEM(w.shape, F32) for w in little]
        + [pltpu.VMEM(chars_row.shape, I32)]
        + [pltpu.VMEM(small.shape, BF) for small in smalls]
        + [
            pltpu.SemaphoreType.DMA((len(big), layers)),
            pltpu.SemaphoreType.DMA((len(shapes),)),
            pltpu.SemaphoreType.DMA((len(EARLY),)),
            pltpu.SemaphoreType.DMA((len(big), layers)),
            pltpu.SemaphoreType.DMA((3,)),
            pltpu.SemaphoreType.DMA((1 + len(smalls),)),
            pltpu.SemaphoreType.DMA((len(little),)),
        ],
        name="backward",
        mib=60,
    )
    act, eg, g1, b1, g2, b2, ub, tg, qg, og, ug, dg = outs
    return act, (eg, g1, b1, tg, qg, og, g2, b2, ug, ub, dg)


def per_device(chars, timesteps, *rest):
    weights, cotangent = rest[:-1], rest[-1]
    width = weights[0].shape[1]
    n_dp, n_blk = lax.axis_size("dp"), lax.axis_size("blk")
    seq = lax.axis_index("dp")
    positions = chars.shape[0]
    chars_row = chars.reshape(1, positions)
    big = [weights[i] for i in (3, 4, 5, 8, 10)]
    counts, sums = call(
        lambda *refs: local_sums(*refs, shares=n_blk),
        [
            jax.ShapeDtypeStruct((n_dp * n_blk, 1, 2 * KPAD), F32),
            jax.ShapeDtypeStruct((SLOT, width), F32),
        ],
        (
            far(chars_row),
            far(cotangent.reshape(positions, width)),
            (seq % GROUP).astype(I32).reshape(1),
            timesteps,
        ),
        [vmem(), vmem(), smem(), smem()],
        [vmem(), vmem()],
        name="local_sums",
    )
    counts = lax.all_to_all(counts, ("dp", "blk"), split_axis=0, concat_axis=0, tiled=True)
    parts = [sums] + [
        lax.ppermute(sums, "blk", [(i, (i + step) % n_blk) for i in range(n_blk)])
        for step in range(1, n_blk)
    ]
    table = call(
        spread_sums,
        jax.ShapeDtypeStruct((n_dp, SLOT, width), BF),
        parts,
        [vmem()] * len(parts),
        vmem(),
        name="spread_sums",
    )
    table = lax.all_to_all(table, "dp", split_axis=0, concat_axis=0, tiled=True)
    scale = 1.0 / (n_dp * n_blk)
    if n_dp == CHUNK:
        kept = run_forward(counts, weights, big)
        act, grads = run_backward(seq.reshape(1).astype(I32), chars_row, table, weights, big, kept, scale)
    else:

        def step(carry, chunk):
            act, grads = carry
            place = seq - chunk * CHUNK
            inside = (place >= 0) & (place < CHUNK)
            here = lax.dynamic_slice_in_dim(counts, chunk * CHUNK * n_blk, CHUNK * n_blk, axis=0)
            part = lax.dynamic_slice_in_dim(table, chunk * CHUNK, CHUNK, axis=0)
            own = jnp.clip(place, 0, CHUNK - 1).reshape(1).astype(I32)
            kept = run_forward(here, weights, big)
            new_act, new_grads = run_backward(own, chars_row, part, weights, big, kept, scale)
            return (jnp.where(inside, new_act, act), tuple(a + b for a, b in zip(grads, new_grads))), None

        start = (jnp.zeros((positions, width), BF), tuple(jnp.zeros(w.shape, F32) for w in weights))
        (act, grads), _ = lax.scan(step, start, jnp.arange(n_dp // CHUNK, dtype=I32))
    return (act.reshape(positions, 1, width), *grads)


def solution(mesh):
    in_specs = (P("blk", "dp"), P("dp")) + (P(),) * 11 + (P("blk", "dp", None),)
    out_specs = (P("blk", "dp", None),) + (P(),) * 11
    return jax.shard_map(
        per_device, mesh=mesh, in_specs=in_specs, out_specs=out_specs, check_vma=False
    )
```

```python
import math
from types import SimpleNamespace

import jax
import jax.numpy as jnp
from jax import lax
from jax.experimental import pallas as pl
from jax.experimental.pallas import tpu as pltpu
from jax.sharding import PartitionSpec as P

HEADS = 8
HEAD = 64
ROWS = 28
GROUP = 4
GROWS = ROWS * GROUP
CHUNK = 16
NROWS = ROWS * CHUNK
NGROUPS = CHUNK // GROUP
KPAD = 128
SLOT = 32
PIECE = 512
HALF = NROWS // 2
MASKED = -1e30
BF = jnp.bfloat16
F32 = jnp.float32
I32 = jnp.int32
MIB = 2**20
DEPTH = 2
GSTRIP = 112
NSTRIP = 112
WIDE = 256
BAND = 512
PER_TASK = 1


def nn(a, b):
    return lax.dot_general(a, b, (((1,), (0,)), ((), ())), preferred_element_type=F32)


def nt(a, b):
    return lax.dot_general(a, b, (((1,), (1,)), ((), ())), preferred_element_type=F32)


def tn(a, b):
    return lax.dot_general(a, b, (((0,), (0,)), ((), ())), preferred_element_type=F32)


def iota(shape, dim):
    return lax.broadcasted_iota(I32, shape, dim)


def hi_lo(values):
    high = values.astype(BF)
    return high, (values - high.astype(F32)).astype(BF)


def row_seq(index):
    return lax.shift_right_logical(index * (65536 // ROWS + 1), 16)


def local_sums(chars_ref, cot_ref, place_ref, time_ref, count_ref, sum_ref, *, shares):
    positions = chars_ref.shape[1]
    chars = chars_ref[...]
    placed = (chars + place_ref[0] * ROWS == iota((KPAD, positions), 0)).astype(F32)
    counts = nt(jnp.ones((8, positions), BF), placed.astype(BF))[0:1]
    stamp = jnp.full((1, KPAD), time_ref[0].astype(F32) * (1.0 / shares), F32)
    row = jnp.concatenate([counts, stamp], axis=1)
    for device in range(count_ref.shape[0]):
        count_ref[device] = row
    onehot = (chars == iota((SLOT, positions), 0)).astype(F32)
    sum_ref[...] = nn(onehot.astype(BF), cot_ref[...])


def spread_sums(*refs):
    *parts, embed, g1, b1, g2, b2, eb, out, pack = refs
    total = parts[0][...]
    for ref in parts[1:]:
        total = total + ref[...]
    total = total.astype(BF)
    for device in range(out.shape[0]):
        out[device] = total
    layers, width = g1.shape
    row = 0
    for ref in (g1, b1, g2, b2, eb):
        for layer in range(layers):
            for start in range(0, ref.shape[1], width):
                pack[row : row + 1, :] = ref[layer : layer + 1, start : start + width].astype(F32)
                row += 1
    pack[row : row + embed.shape[0], :] = embed[...].astype(F32)


class Loads:
    def __init__(self, depth):
        self.depth, self.queue, self.done = depth, [], set()

    def add(self, key, source, target, sem):
        self.queue.append((key, pltpu.make_async_copy(source, target, sem)))

    def begin(self):
        self.started = 0
        self.advance(self.depth)

    def need(self, *keys):
        for key in keys:
            while key not in self.done:
                if len(self.done) == self.started:
                    self.advance(1)
                first, copy = self.queue[len(self.done)]
                copy.wait()
                self.done.add(first)

    def advance(self, count):
        for _, copy in self.queue[self.started : self.started + count]:
            copy.start()
        self.started = min(self.started + count, len(self.queue))


def normalise(values):
    mean = jnp.mean(values, axis=-1, keepdims=True)
    centered = values - mean
    rstd = lax.rsqrt(jnp.mean(centered * centered, axis=-1, keepdims=True) + 1e-05)
    return centered * rstd, rstd


def norm_back(grad_out, unit, rstd, gain):
    scaled = grad_out * gain
    return rstd * (
        scaled
        - jnp.mean(scaled, axis=-1, keepdims=True)
        - unit * jnp.mean(scaled * unit, axis=-1, keepdims=True)
    )


def gelu_and_slope(up):
    size = jnp.abs(up)
    bell = jnp.exp2((-0.5 / math.log(2.0)) * (up * up))
    shift = math.sqrt(2.0) / 0.3275911
    ratio = 1.0 / (shift + size)
    poly = 0.5 * shift**5 * 1.061405429
    for power, term in ((4, -1.453152027), (3, 1.421413741), (2, -0.284496736), (1, 0.254829592)):
        poly = poly * ratio + 0.5 * shift**power * term
    tail = (poly * ratio) * bell
    slope = tail - (size * bell) * (1.0 / math.sqrt(2 * math.pi))
    return jnp.maximum(up, 0.0) - size * tail, jnp.where(up > 0, 1.0 - slope, slope)


def row_choices():
    row = iota((NROWS, 1), 0)
    seq_of = row_seq(row)
    char_of = row - seq_of * ROWS
    pick_char = (char_of == iota((NROWS, SLOT), 1)).astype(F32).astype(BF)
    pick_seq = (seq_of == iota((NROWS, CHUNK), 1)).astype(F32).astype(BF)
    return seq_of, char_of, pick_char, pick_seq


def side_masks():
    left = (iota((GROWS, KPAD), 1) < HEAD).astype(F32)
    return left.astype(BF), (1.0 - left).astype(BF)


def blocks(qkv, masks, group, pair, part):
    lanes = part * (qkv.shape[1] // 3) + pair * KPAD
    both = qkv[group * GROWS : (group + 1) * GROWS, lanes : lanes + KPAD]
    return jnp.concatenate([both * masks[0], both * masks[1]], axis=0)


def wide(rows, layer):
    pack, first = rows
    return pack[first + layer : first + layer + 1, :]


def small_rows(pack, layers, pieces):
    firsts = dict(g1=0, b1=layers, g2=2 * layers, b2=3 * layers, eb=4 * layers, embed=(4 + pieces) * layers)
    return SimpleNamespace(**{name: (pack, first) for name, first in firsts.items()})


EARLY = ("unit1", "rstd1", "norm1", "qkv", "probs")
KEPT = ("unit1", "rstd1", "norm1", "qkv", "probs", "att", "unit2", "rstd2", "norm2", "hid", "slp")


def kept_shapes(width, inner):
    row = {"rstd1": (KPAD, F32), "rstd2": (KPAD, F32), "qkv": (3 * width, BF), "hid": (inner, BF), "slp": (inner, BF)}
    shapes = {name: ((NROWS, row.get(name, (width, BF))[0]), row.get(name, (width, BF))[1]) for name in KEPT}
    shapes["probs"] = ((NGROUPS, HEADS // 2, 2 * GROWS, GROWS), BF)
    return [shapes[name] for name in KEPT]


def halves(size=HALF):
    return [slice(start, start + size) for start in range(0, NROWS, size)]


def strips(span, rows):
    return [slice(start, start + rows) for start in range(span.start, span.stop, rows)]


def groups_of(span):
    return range(span.start // GROWS, span.stop // GROWS)


def forward_tasks(layer, small, weight, kept, source, xs, mid, bias, masks, need, shifted=None):
    width = xs.shape[1]
    inner = kept.hid.shape[1]
    pairs = width // KPAD

    def normed(span, values, unit_ref, rstd_ref, norm_ref, gain, shift):
        unit, rstd = normalise(values[span, :])
        unit_ref[span, :] = unit.astype(BF)
        rstd_ref[span, :] = jnp.broadcast_to(rstd, (rstd.shape[0], KPAD))
        norm_ref[span, :] = (unit * wide(gain, layer) + wide(shift, layer)).astype(BF)

    def ln1(span):
        normed(span, source, kept.unit1, kept.rstd1, kept.norm1, small.g1, small.b1)

    def qkv(span):
        need("q")
        for part in range(3):
            lanes = slice(part * width, (part + 1) * width)
            product = nn(kept.norm1[span, :], weight.q[:, lanes])
            kept.qkv[span, lanes] = (product * 0.125 if part == 0 else product).astype(BF)

    def attend(span):
        for group in groups_of(span):
            rows = slice(group * GROWS, (group + 1) * GROWS)
            lanes = [slice(pair * KPAD, (pair + 1) * KPAD) for pair in range(pairs)]
            scores = [
                nt(blocks(kept.qkv, masks, group, pair, 1), kept.qkv[rows, lanes[pair]]) for pair in range(pairs)
            ]
            yield
            for pair in range(pairs):
                for side in range(2):
                    keys = slice(side * GROWS, (side + 1) * GROWS)
                    score = scores[pair][keys] + bias[group]
                    heft = jnp.exp(score - jnp.max(score, axis=0, keepdims=True))
                    prob = heft * (1.0 / jnp.sum(heft, axis=0, keepdims=True))
                    kept.probs[group, pair, keys, :] = prob.astype(BF)
            yield
            for pair in range(pairs):
                kept.att[rows, lanes[pair]] = tn(
                    kept.probs[group, pair], blocks(kept.qkv, masks, group, pair, 2)
                ).astype(BF)
            yield

    def out(span):
        need("o")
        mid[span, :] = source[span, :] + nn(kept.att[span, :], weight.o[...])

    def ln2(span):
        normed(span, mid, kept.unit2, kept.rstd2, kept.norm2, small.g2, small.b2)

    def up(span):
        need("e")
        for piece in range(inner // PIECE):
            cols = slice(piece * PIECE, (piece + 1) * PIECE)
            product = nn(kept.norm2[span, :], weight.e[:, cols])
            shift = wide(small.eb, layer * (inner // PIECE) + piece)
            for rows in strips(span, GSTRIP):
                strip = product[rows.start - span.start : rows.stop - span.start]
                hidden, slope = gelu_and_slope(strip + shift)
                kept.hid[rows, cols] = hidden.astype(BF)
                kept.slp[rows, cols] = slope.astype(BF)
                yield

    def down(span):
        need("c")
        for start in range(0, width, WIDE):
            cols = slice(start, start + WIDE)
            total = mid[span, cols] + nn(kept.hid[span, :], weight.c[:, cols])
            xs[span, cols] = total if shifted is None else total + shifted[span, cols]
            yield

    parts = dict(ln1=ln1, qkv=qkv, attend=attend, out=out, ln2=ln2, up=up, down=down)
    return {
        f"{name}{half}": (lambda part=part, span=span: part(span))
        for name, part in parts.items()
        for half, span in enumerate(halves())
    }


def backward_tasks(layer, small, weight, kept, work, masks, need, send, features, picks, grads):
    xs, mid, acc = work.xs, work.mid, work.acc
    width = xs.shape[1]
    inner = kept.hid.shape[1]
    pairs = width // KPAD
    left_lanes = iota((GROWS, KPAD), 1) < HEAD

    def add_rows(ref, span, value, cols=slice(None)):
        total = jnp.sum(value, axis=0, keepdims=True)
        ref[layer : layer + 1, cols] = total if span.start == 0 else ref[layer : layer + 1, cols] + total

    def grad_up(span):
        need("c", "slp")
        for piece in range(inner // PIECE):
            cols = slice(piece * PIECE, (piece + 1) * PIECE)
            value = nt(work.gff[span, :], weight.c[cols, :]) * kept.slp[span, cols].astype(F32)
            add_rows(grads.ub, span, value, cols)
            work.gu[span, cols] = value.astype(BF)

    def grad_norm2(span):
        need("e")
        acc[span, :] = nt(work.gu[span, :], weight.e[...])

    def ln2_back(span):
        need("unit2", "rstd2")
        for rows in strips(span, NSTRIP):
            unit, grad = kept.unit2[rows, :].astype(F32), acc[rows, :]
            add_rows(grads.g2, rows, grad * unit)
            add_rows(grads.b2, rows, grad)
            total = xs[rows, :] + norm_back(grad, unit, kept.rstd2[rows, 0:1], wide(small.g2, layer))
            mid[rows, :] = total
            work.gb[rows, :] = total.astype(BF)
            yield

    def grad_att(span):
        need("o")
        work.ga[span, :] = nt(work.gb[span, :], weight.o[...]).astype(BF)

    def attend_back(span):
        need("qkv", "probs")
        for group in groups_of(span):
            rows = slice(group * GROWS, (group + 1) * GROWS)
            lanes = [slice(pair * KPAD, (pair + 1) * KPAD) for pair in range(pairs)]
            grad_probs = [
                nt(blocks(kept.qkv, masks, group, pair, 2), work.ga[rows, lanes[pair]]) for pair in range(pairs)
            ]
            yield
            for pair in range(pairs):
                for side in range(2):
                    keys = slice(side * GROWS, (side + 1) * GROWS)
                    prob = kept.probs[group, pair, keys, :].astype(F32)
                    grad_prob = grad_probs[pair][keys]
                    delta = jnp.sum(prob * grad_prob, axis=0, keepdims=True)
                    work.gscore[pair, keys, :] = (prob * (grad_prob - delta)).astype(BF)
            yield
            for pair in range(pairs):
                grad_score = work.gscore[pair]
                work.gproj[rows, lanes[pair]] = (
                    tn(grad_score, blocks(kept.qkv, masks, group, pair, 1)) * 0.125
                ).astype(BF)
                grad_key = nn(grad_score, kept.qkv[rows, lanes[pair]])
                grad_value = nn(kept.probs[group, pair], work.ga[rows, lanes[pair]])
                for part, product in ((1, grad_key), (2, grad_value)):
                    joined = jnp.where(left_lanes, product[0:GROWS], product[GROWS : 2 * GROWS])
                    start = part * width + pair * KPAD
                    work.gproj[rows, start : start + KPAD] = joined.astype(BF)
            yield

    def grad_norm1(span):
        need("q")
        acc[span, :] = nt(work.gproj[span, :], weight.q[...])

    def ln1_back(span):
        need("unit1", "rstd1")
        for rows in strips(span, NSTRIP):
            unit, grad = kept.unit1[rows, :].astype(F32), acc[rows, :]
            add_rows(grads.g1, rows, grad * unit)
            add_rows(grads.b1, rows, grad)
            total = mid[rows, :] + norm_back(grad, unit, kept.rstd1[rows, 0:1], wide(small.g1, layer))
            xs[rows, :] = total
            work.gff[rows, :] = total.astype(BF)
            yield

    def down_term():
        need("hid")
        yield from send("down", layer, kept.hid, work.gff)

    def up_term():
        need("norm2")
        yield from send("up", layer, kept.norm2, work.gu)

    def out_term():
        need("att")
        yield from send("out", layer, kept.att, work.gb)

    def qkv_term():
        need("norm1")
        yield from send("qkv", layer, kept.norm1, work.gproj)

    def time_term():
        pick_char, pick_seq = picks
        by_seq = tn(pick_seq, work.gff[...]).astype(BF)
        yield from send("time", layer, features, by_seq)
        if layer == 0:
            grads.eg[...] = tn(pick_char, work.gff[...])[0 : grads.eg.shape[0]]

    by_half = dict(
        grad_up=grad_up, grad_norm2=grad_norm2, ln2_back=ln2_back, grad_att=grad_att,
        attend_back=attend_back, grad_norm1=grad_norm1, ln1_back=ln1_back,
    )
    tasks = {
        f"{name}{half}": (lambda part=part, span=span: part(span))
        for name, part in by_half.items()
        for half, span in enumerate(halves(NROWS))
    }
    tasks.update(down_term=down_term, up_term=up_term, out_term=out_term, qkv_term=qkv_term, time_term=time_term)
    return tasks


FIRST_ORDER = (
    "ln10", "ln11", "qkv0", "qkv1", "attend0", "attend1", "out0", "out1", "shift0", "ln20", "ln21", "up0", "up1",
    "down0", "down1",
)
SECOND_ORDER = ("ln10", "ln11", "qkv0", "qkv1", "attend0", "attend1")
LATTER_ORDER = ("out0", "out1", "ln20", "ln21", "up0", "down0|up1", "down1")
FORWARD_ORDER = (
    "ln10", "ln11", "qkv0", "qkv1", "attend0", "out0", "ln20", "attend1|up0", "out1", "ln21", "down0|up1", "down1",
)
BACKWARD_ORDER = (
    "grad_up0", "down_term", "grad_norm20", "ln2_back0|up_term", "grad_att0", "attend_back0|out_term", "grad_norm10",
    "ln1_back0|qkv_term", "time_term",
)


def bring(sources, targets, sems):
    copies = [pltpu.make_async_copy(a, b, sems.at[i]) for i, (a, b) in enumerate(zip(sources, targets))]
    for copy in copies:
        copy.start()
    return copies


def run_parts(names, tasks):
    steps = [step for step in (tasks[name]() for name in names.split("|")) if step is not None]
    while steps:
        steps = [step for step in steps if next(step, steps) is not steps]


def run_tasks(order, tasks, loads):
    for names in order:
        run_parts(names, tasks)
        loads.advance(PER_TASK)


def time_shift(features, weight, pick_seq):
    return nn(jnp.concatenate([pick_seq, pick_seq], axis=1), jnp.concatenate(hi_lo(nn(features, weight)), axis=0))


def first_layer(
    counts_ref, pack_ref,
    wt_hbm, wq_hbm, wo_hbm, we_hbm, wc_hbm,
    feat_ref, xs, next_att, next_o, *rest, vocab
):
    count = len(KEPT)
    kept_hbm, early_hbm, rest = rest[:count], rest[count : count + len(EARLY)], rest[count + len(EARLY) :]
    weight = SimpleNamespace(**dict(zip("tqoec", rest[:5])))
    kept_refs, rest = rest[5 : 5 + count], rest[5 + count :]
    kept = SimpleNamespace(**dict(zip(KEPT, kept_refs)))
    early_refs, rest = rest[: len(EARLY)], rest[len(EARLY) :]
    early = SimpleNamespace(att=next_att, hid=kept.hid, **dict(zip(EARLY, early_refs)))
    later, next_q, bias, mid, shifted, in_sem, out_sem, early_sem = rest
    width = xs.shape[1]
    small = small_rows(pack_ref, wt_hbm.shape[0], kept.hid.shape[1] // PIECE)
    loads = Loads(2)
    for index, (name, source) in enumerate(zip("tqoec", (wt_hbm, wq_hbm, wo_hbm, we_hbm, wc_hbm))):
        loads.add(name, source.at[0], getattr(weight, name), in_sem.at[index])
        if name == "o":
            loads.add("later", wt_hbm.at[1], later, in_sem.at[5])
    loads.add("next_q", wq_hbm.at[1], next_q, in_sem.at[6])
    loads.add("next_o", wo_hbm.at[1], next_o, in_sem.at[7])
    loads.begin()
    pushed = []

    def push(half, names, sources, targets, sems, wanted):
        for name in wanted:
            index = names.index(name)
            unit = GROWS if name == "probs" else 1
            rows = pl.ds(half * HALF // unit, HALF // unit)
            pushed.append(
                pltpu.make_async_copy(sources[index].at[rows], targets[index].at[rows], sems.at[index, half])
            )
            pushed[-1].start()

    _, _, pick_char, pick_seq = row_choices()
    masks = side_masks()

    shares = counts_ref.shape[0] // CHUNK
    stamp = []
    for group in range(NGROUPS):
        total = jnp.zeros((1, KPAD), F32)
        for member in range(GROUP):
            value = jnp.zeros((1, 2 * KPAD), F32)
            for share in range(shares):
                value = value + counts_ref[(group * GROUP + member) * shares + share]
            total = total + value[:, 0:KPAD]
            stamp.append(value[:, KPAD:])
        same = row_seq(iota((GROWS, GROWS), 1)) == row_seq(iota((GROWS, GROWS), 0))
        counts = jnp.broadcast_to(total[:, 0:GROWS], (GROWS, GROWS)).T
        live = same & (counts > 0.5)
        bias[group] = jnp.where(live, jnp.log(jnp.maximum(counts, 1.0)), MASKED)
    times = jnp.concatenate(stamp, axis=0)
    half = width // 2
    cycles = [
        times * jnp.exp((iota((1, KPAD), 1) + start).astype(F32) * (-math.log(10000.0) / half))
        for start in range(0, half, KPAD)
    ]
    features = jnp.concatenate(
        [jnp.sin(phase) for phase in cycles] + [jnp.cos(phase) for phase in cycles], axis=1
    ).astype(BF)
    feat_ref[...] = features
    loads.need("t")
    embed = pack_ref[small.embed[1] : small.embed[1] + vocab, :].astype(BF)
    xs[...] = nn(pick_char[:, 0:vocab], embed) + time_shift(features, weight.t[...], pick_seq)
    tasks = forward_tasks(0, small, weight, kept, xs, xs, mid, bias, masks, loads.need, shifted)

    def shift_next():
        loads.need("later")
        shifted[...] = time_shift(features, later[...], pick_seq)

    tasks["shift0"] = shift_next
    after = {"ln1": ("unit1", "rstd1", "norm1"), "qkv": ("qkv",), "attend": ("probs", "att"),
             "ln2": ("unit2", "rstd2", "norm2"), "up": ("hid", "slp")}
    second = forward_tasks(
        1, small, SimpleNamespace(q=next_q, o=next_o), early, xs, xs, mid, bias, masks,
        lambda name: loads.need("next_" + name),
    )
    for order, work, target in (
        (FIRST_ORDER, tasks, (KEPT, kept_refs, kept_hbm, out_sem)),
        (SECOND_ORDER, second, (EARLY, early_refs, early_hbm, early_sem)),
    ):
        for names in order:
            run_parts(names, work)
            loads.advance(PER_TASK)
            for name in names.split("|"):
                wanted = [array for array in after.get(name[:-1], ()) if array in target[0]]
                push(int(name[-1]), *target, wanted)
    loads.need("next_o")
    for copy in pushed:
        copy.wait()


def other_layers(
    own_ref, feat_ref, x_ref, att_ref, o_ref, pack_ref, chars_hbm,
    table_hbm, wt_hbm, wq_hbm, wo_hbm, we_hbm, wc_hbm, *rest, scale
):
    count = len(KEPT)
    layers, width = wq_hbm.shape[:2]
    kept_hbm, early_hbm, rest = rest[:count], rest[count : count + len(EARLY)], rest[count + len(EARLY) :]
    act_hbm, *little_hbm = rest[:7]
    outs = dict(zip(("time", "qkv", "out", "up", "down"), rest[7:12]))
    rest = rest[12:]
    weights, kept = [], []
    for layer in range(layers):
        weights.append(SimpleNamespace(**dict(zip("tqoec", rest[:5]))))
        kept.append(SimpleNamespace(**dict(zip(KEPT, rest[5 : 5 + count]))))
        rest = rest[5 + count :]
    weights[1].o, kept[1].att = o_ref, att_ref
    names = ("xs", "mid", "acc", "ga", "gproj", "gscore", "gu", "gb", "gff", "end", "act", "table")
    work = SimpleNamespace(**dict(zip(names, rest)))
    rest = rest[len(names) :]
    stages = dict(zip(outs, rest[:5]))
    little, rest = rest[5:11], rest[11:]
    chars_ref, rest = rest[0], rest[1:]
    in_sem, kept_sem, early_sem, out_sem, end_sem, small_sem, little_sem = rest
    eg, g1g, b1g, g2g, b2g, ubg = little
    xs, mid = work.xs, work.mid
    small = small_rows(pack_ref, layers, kept[0].hid.shape[1] // PIECE)
    (chars_copy,) = bring((chars_hbm,), (chars_ref,), small_sem)
    grads = SimpleNamespace(eg=eg, g1=g1g, b1=b1g, g2=g2g, b2=b2g, ub=ubg)
    sources = dict(zip("tqoec", (wt_hbm, wq_hbm, wo_hbm, we_hbm, wc_hbm)))
    loads = Loads(DEPTH)
    for layer in range(1, layers):
        for name in "ec" if layer == 1 else "tqoec":
            loads.add(
                (layer, name), sources[name].at[layer], getattr(weights[layer], name), in_sem.at["tqoec".index(name), layer]
            )
    for name in ("probs", "qkv", "norm1", "q", "unit1", "rstd1"):
        if name in EARLY:
            index = EARLY.index(name)
            loads.add((1, name), early_hbm[index], getattr(kept[1], name), early_sem.at[index])
        else:
            loads.add((1, name), sources[name].at[1], weights[1].q, in_sem.at["tqoec".index(name), 1])
    for name in ("slp", "c", "hid", "e", "norm2", "unit2", "rstd2", "o", "att", "probs", "qkv", "q", "norm1", "unit1", "rstd1"):
        if name in KEPT:
            index = KEPT.index(name)
            loads.add((0, name), kept_hbm[index], getattr(kept[0], name), kept_sem.at[index])
        else:
            loads.add((0, name), sources[name].at[0], getattr(weights[0], name), in_sem.at["tqoec".index(name), 0])
    loads.begin()
    table_copy = pltpu.make_async_copy(table_hbm, work.table, end_sem.at[2])
    table_copy.start()
    queued = {key for key, _ in loads.queue}

    def needs(layer):
        return lambda *names: loads.need(*((layer, name) for name in names if (layer, name) in queued))

    seq_of, char_of, pick_char, pick_seq = row_choices()
    masks = side_masks()
    features = feat_ref[...]
    for layer in range(1, layers):
        source, order = (x_ref, LATTER_ORDER) if layer == 1 else (xs, FORWARD_ORDER)
        if layer > 1:
            needs(layer)("t")
            xs[...] = xs[...] + time_shift(features, weights[layer].t[...], pick_seq)
        run_tasks(
            order,
            forward_tasks(layer, small, weights[layer], kept[layer], source, xs, mid, None, masks, needs(layer)),
            loads,
        )

    own = own_ref[0]
    work.end[0:NROWS, :] = xs[...].astype(BF)
    work.end[NROWS:, :] = jnp.zeros((work.end.shape[0] - NROWS, width), BF)
    chars_copy.wait()
    place = chars_ref[...] + lax.rem(own, GROUP) * ROWS
    hot = (place == iota((KPAD, chars_ref.shape[1]), 0)).astype(F32).astype(BF)
    start = pl.multiple_of(lax.div(own, GROUP) * GROWS, 16)
    work.act[...] = tn(hot, work.end[pl.ds(start, KPAD), :]).astype(BF)
    act_copy = pltpu.make_async_copy(work.act, act_hbm, end_sem.at[1])
    act_copy.start()

    table_copy.wait()
    for seq in range(CHUNK):
        xs[seq * ROWS : (seq + 1) * ROWS, :] = work.table[seq].astype(F32)[0:ROWS] * scale
    work.gff[...] = xs[...].astype(BF)

    sends = {}

    def send(name, layer, left, right):
        if name in sends:
            sends.pop(name).wait()
        stage = stages[name]
        for start in range(0, stage.shape[0], BAND):
            stage[start : start + BAND, :] = tn(left[:, start : start + BAND], right[...])
            yield
        copy = pltpu.make_async_copy(stage, outs[name].at[layer], out_sem.at[list(outs).index(name), layer])
        copy.start()
        sends[name] = copy

    for layer in reversed(range(layers)):
        run_tasks(
            BACKWARD_ORDER,
            backward_tasks(layer, small, weights[layer], kept[layer], work, masks, needs(layer), send,
                           features, (pick_char, pick_seq), grads),
            loads,
        )
    finals = bring(little, little_hbm, little_sem)
    act_copy.wait()
    for copy in [*sends.values(), *finals]:
        copy.wait()


def vmem():
    return pl.BlockSpec(memory_space=pltpu.VMEM)


def smem():
    return pl.BlockSpec(memory_space=pltpu.SMEM)


def anywhere():
    return pl.BlockSpec(memory_space=pl.ANY)


def call(body, outs, ins, in_specs, out_specs, scratch=(), name=None, mib=8):
    return pl.pallas_call(
        body,
        out_shape=outs,
        in_specs=in_specs,
        out_specs=out_specs,
        scratch_shapes=list(scratch),
        compiler_params=pltpu.CompilerParams(vmem_limit_bytes=mib * MIB),
        name=name,
    )(*ins)


def far(array):
    return pltpu.with_memory_space_constraint(array, pltpu.HBM)


def keep(array):
    return pltpu.with_memory_space_constraint(array, pltpu.VMEM)


def run_forward(counts, pack, weights, big):
    embed, expand_bias = weights[0], weights[9]
    width, inner = embed.shape[1], expand_bias.shape[1]
    shapes = kept_shapes(width, inner)
    early = [shapes[KEPT.index(name)] for name in EARLY]
    table = (NROWS, width)
    return call(
        lambda *refs: first_layer(*refs, vocab=embed.shape[0]),
        [
            pltpu.VMEM((CHUNK, width), BF),
            pltpu.VMEM(table, F32),
            pltpu.VMEM(table, BF),
            pltpu.VMEM(big[2].shape[1:], BF),
        ]
        + [pltpu.HBM(shape, dtype) for shape, dtype in shapes + early],
        (counts, keep(pack), *map(far, big)),
        [vmem()] * 2 + [anywhere()] * len(big),
        [vmem()] * 4 + [anywhere()] * (len(shapes) + len(early)),
        [pltpu.VMEM(w.shape[1:], w.dtype) for w in big]
        + [pltpu.VMEM(shape, dtype) for shape, dtype in shapes + early]
        + [
            pltpu.VMEM(big[0].shape[1:], BF),
            pltpu.VMEM(big[1].shape[1:], BF),
            pltpu.VMEM((NGROUPS, GROWS, GROWS), F32),
            pltpu.VMEM(table, F32),
            pltpu.VMEM(table, F32),
            pltpu.SemaphoreType.DMA((len(big) + 3,)),
            pltpu.SemaphoreType.DMA((len(shapes), NROWS // HALF)),
            pltpu.SemaphoreType.DMA((len(early), NROWS // HALF)),
        ],
        name="forward",
        mib=40,
    )


def run_backward(own, chars_row, pack, table, weights, big, passed, scale):
    (embed, ln1_gain, ln1_bias, w_time, w_qkv, w_out, ln2_gain, ln2_bias, expand_weight, expand_bias,
     contract_weight) = weights
    layers, width = ln1_gain.shape
    inner = expand_bias.shape[1]
    shapes = kept_shapes(width, inner)
    positions = chars_row.shape[1]
    whole = (NROWS, width)

    def f32_like(array):
        return jax.ShapeDtypeStruct(array.shape, F32)

    features, x, att, next_o, *kept = passed
    layer_scratch = [pltpu.VMEM(w.shape[1:], w.dtype) for w in big] + [
        pltpu.VMEM(shape, dtype) for shape, dtype in shapes
    ]
    smalls = (ln1_gain, ln1_bias, ln2_gain, ln2_bias, expand_bias)
    little = (embed, *smalls)
    outs = call(
        lambda *refs: other_layers(*refs, scale=scale),
        [jax.ShapeDtypeStruct((positions, width), BF)]
        + [f32_like(w) for w in (*little, w_time, w_qkv, w_out, expand_weight, contract_weight)],
        (own, keep(features), keep(x), keep(att), keep(next_o), keep(pack), far(chars_row), keep(table), *map(far, big),
         *map(far, kept)),
        [smem()] + [vmem()] * 5 + [anywhere()] * (2 + len(big) + len(kept)),
        [anywhere()] * 12,
        layer_scratch * layers
        + [
            pltpu.VMEM(whole, F32),
            pltpu.VMEM(whole, F32),
            pltpu.VMEM(whole, F32),
            pltpu.VMEM(whole, BF),
            pltpu.VMEM((NROWS, 3 * width), BF),
            pltpu.VMEM((HEADS // 2, 2 * GROWS, GROWS), BF),
            pltpu.VMEM((NROWS, inner), BF),
            pltpu.VMEM(whole, BF),
            pltpu.VMEM(whole, BF),
            pltpu.VMEM((NROWS + KPAD - GROWS, width), BF),
            pltpu.VMEM((positions, width), BF),
            pltpu.VMEM(table.shape, BF),
        ]
        + [pltpu.VMEM(w.shape[1:], F32) for w in big]
        + [pltpu.VMEM(w.shape, F32) for w in little]
        + [pltpu.VMEM(chars_row.shape, I32)]
        + [
            pltpu.SemaphoreType.DMA((len(big), layers)),
            pltpu.SemaphoreType.DMA((len(shapes),)),
            pltpu.SemaphoreType.DMA((len(EARLY),)),
            pltpu.SemaphoreType.DMA((len(big), layers)),
            pltpu.SemaphoreType.DMA((3,)),
            pltpu.SemaphoreType.DMA((1,)),
            pltpu.SemaphoreType.DMA((len(little),)),
        ],
        name="backward",
        mib=60,
    )
    act, eg, g1, b1, g2, b2, ub, tg, qg, og, ug, dg = outs
    return act, (eg, g1, b1, tg, qg, og, g2, b2, ug, ub, dg)


def per_device(chars, timesteps, *rest):
    weights, cotangent = rest[:-1], rest[-1]
    width = weights[0].shape[1]
    n_dp, n_blk = lax.axis_size("dp"), lax.axis_size("blk")
    seq = lax.axis_index("dp")
    positions = chars.shape[0]
    chars_row = chars.reshape(1, positions)
    big = [weights[i] for i in (3, 4, 5, 8, 10)]
    counts, sums = call(
        lambda *refs: local_sums(*refs, shares=n_blk),
        [
            pltpu.VMEM((n_dp * n_blk, 1, 2 * KPAD), F32),
            pltpu.VMEM((SLOT, width), F32),
        ],
        (
            far(chars_row),
            far(cotangent.reshape(positions, width)),
            (seq % GROUP).astype(I32).reshape(1),
            timesteps,
        ),
        [vmem(), vmem(), smem(), smem()],
        [vmem(), vmem()],
        name="local_sums",
    )
    counts = lax.all_to_all(counts, ("dp", "blk"), split_axis=0, concat_axis=0, tiled=True)
    parts = [sums] + [
        lax.ppermute(sums, "blk", [(i, (i + step) % n_blk) for i in range(n_blk)])
        for step in range(1, n_blk)
    ]
    embed, ln1_gain, ln1_bias, _, _, _, ln2_gain, ln2_bias, _, expand_bias, _ = weights
    smalls = (embed, ln1_gain, ln1_bias, ln2_gain, ln2_bias, expand_bias)
    pack_rows = sum(w.size for w in smalls) // width
    table, pack = call(
        spread_sums,
        [
            pltpu.VMEM((n_dp, SLOT, width), BF) if n_dp == CHUNK else jax.ShapeDtypeStruct((n_dp, SLOT, width), BF),
            pltpu.VMEM((pack_rows + -pack_rows % 8, width), F32),
        ],
        (*parts, *map(far, smalls)),
        [vmem()] * (len(parts) + len(smalls)),
        [vmem()] * 2,
        name="spread_sums",
    )
    table = lax.all_to_all(table, "dp", split_axis=0, concat_axis=0, tiled=True)
    scale = 1.0 / (n_dp * n_blk)
    if n_dp == CHUNK:
        kept = run_forward(counts, pack, weights, big)
        act, grads = run_backward(seq.reshape(1).astype(I32), chars_row, pack, table, weights, big, kept, scale)
    else:

        def step(carry, chunk):
            act, grads = carry
            place = seq - chunk * CHUNK
            inside = (place >= 0) & (place < CHUNK)
            here = lax.dynamic_slice_in_dim(counts, chunk * CHUNK * n_blk, CHUNK * n_blk, axis=0)
            part = lax.dynamic_slice_in_dim(table, chunk * CHUNK, CHUNK, axis=0)
            own = jnp.clip(place, 0, CHUNK - 1).reshape(1).astype(I32)
            kept = run_forward(here, pack, weights, big)
            new_act, new_grads = run_backward(own, chars_row, pack, part, weights, big, kept, scale)
            return (jnp.where(inside, new_act, act), tuple(a + b for a, b in zip(grads, new_grads))), None

        start = (jnp.zeros((positions, width), BF), tuple(jnp.zeros(w.shape, F32) for w in weights))
        (act, grads), _ = lax.scan(step, start, jnp.arange(n_dp // CHUNK, dtype=I32))
    return (act.reshape(positions, 1, width), *grads)


def solution(mesh):
    in_specs = (P("blk", "dp"), P("dp")) + (P(),) * 11 + (P("blk", "dp", None),)
    out_specs = (P("blk", "dp", None),) + (P(),) * 11
    return jax.shard_map(
        per_device, mesh=mesh, in_specs=in_specs, out_specs=out_specs, check_vma=False
    )
```

```python
import math
from types import SimpleNamespace

import jax
import jax.numpy as jnp
from jax import lax
from jax.experimental import pallas as pl
from jax.experimental.pallas import tpu as pltpu
from jax.sharding import PartitionSpec as P

HEADS = 8
HEAD = 64
ROWS = 28
GROUP = 4
GROWS = ROWS * GROUP
CHUNK = 16
NROWS = ROWS * CHUNK
NGROUPS = CHUNK // GROUP
KPAD = 128
SLOT = 32
PIECE = 512
HALF = NROWS // 2
MASKED = -1e30
BF = jnp.bfloat16
F32 = jnp.float32
I32 = jnp.int32
MIB = 2**20
DEPTH = 3
GSTRIP = 112
NSTRIP = 112
WIDE = 256
BAND = 512
PER_TASK = 1


def nn(a, b):
    return lax.dot_general(a, b, (((1,), (0,)), ((), ())), preferred_element_type=F32)


def nt(a, b):
    return lax.dot_general(a, b, (((1,), (1,)), ((), ())), preferred_element_type=F32)


def tn(a, b):
    return lax.dot_general(a, b, (((0,), (0,)), ((), ())), preferred_element_type=F32)


def iota(shape, dim):
    return lax.broadcasted_iota(I32, shape, dim)


def hi_lo(values):
    high = values.astype(BF)
    return high, (values - high.astype(F32)).astype(BF)


def row_seq(index):
    return lax.shift_right_logical(index * (65536 // ROWS + 1), 16)


def local_sums(chars_ref, cot_ref, place_ref, time_ref, count_ref, sum_ref, *, shares):
    positions = chars_ref.shape[1]
    chars = chars_ref[...]
    placed = (chars + place_ref[0] * ROWS == iota((KPAD, positions), 0)).astype(F32)
    counts = nt(jnp.ones((8, positions), BF), placed.astype(BF))[0:1]
    stamp = jnp.full((1, KPAD), time_ref[0].astype(F32) * (1.0 / shares), F32)
    row = jnp.where(iota((1, KPAD), 1) < GROWS, counts, stamp)
    for device in range(count_ref.shape[0]):
        count_ref[device] = row
    onehot = (chars == iota((SLOT, positions), 0)).astype(F32)
    sum_ref[...] = nn(onehot.astype(BF), cot_ref[...])


def spread_sums(*refs):
    *parts, embed, g1, b1, g2, b2, eb, out, pack = refs
    total = parts[0][...]
    for ref in parts[1:]:
        total = total + ref[...]
    total = total.astype(BF)
    for device in range(out.shape[0]):
        out[device] = total
    layers, width = g1.shape
    row = 0
    for ref in (g1, b1, g2, b2, eb):
        for layer in range(layers):
            for start in range(0, ref.shape[1], width):
                pack[row : row + 1, :] = ref[layer : layer + 1, start : start + width].astype(F32)
                row += 1
    pack[row : row + embed.shape[0], :] = embed[...].astype(F32)


class Loads:
    def __init__(self, depth):
        self.depth, self.queue, self.done = depth, [], set()

    def add(self, key, source, target, sem):
        self.queue.append((key, pltpu.make_async_copy(source, target, sem)))

    def begin(self):
        self.started = 0
        self.advance(self.depth)

    def need(self, *keys):
        for key in keys:
            while key not in self.done:
                if len(self.done) == self.started:
                    self.advance(1)
                first, copy = self.queue[len(self.done)]
                copy.wait()
                self.done.add(first)

    def advance(self, count):
        for _, copy in self.queue[self.started : self.started + count]:
            copy.start()
        self.started = min(self.started + count, len(self.queue))


def normalise(values):
    mean = jnp.mean(values, axis=-1, keepdims=True)
    centered = values - mean
    rstd = lax.rsqrt(jnp.mean(centered * centered, axis=-1, keepdims=True) + 1e-05)
    return centered * rstd, rstd


def norm_back(grad_out, unit, rstd, gain):
    scaled = grad_out * gain
    return rstd * (
        scaled
        - jnp.mean(scaled, axis=-1, keepdims=True)
        - unit * jnp.mean(scaled * unit, axis=-1, keepdims=True)
    )


def gelu_and_slope(up):
    size = jnp.abs(up)
    bell = jnp.exp2((-0.5 / math.log(2.0)) * (up * up))
    shift = math.sqrt(2.0) / 0.3275911
    ratio = 1.0 / (shift + size)
    poly = 0.5 * shift**5 * 1.061405429
    for power, term in ((4, -1.453152027), (3, 1.421413741), (2, -0.284496736), (1, 0.254829592)):
        poly = poly * ratio + 0.5 * shift**power * term
    tail = (poly * ratio) * bell
    slope = tail - (size * bell) * (1.0 / math.sqrt(2 * math.pi))
    return jnp.maximum(up, 0.0) - size * tail, jnp.where(up > 0, 1.0 - slope, slope)


def row_choices():
    row = iota((NROWS, 1), 0)
    seq_of = row_seq(row)
    char_of = row - seq_of * ROWS
    pick_char = (char_of == iota((NROWS, SLOT), 1)).astype(F32).astype(BF)
    pick_seq = (seq_of == iota((NROWS, CHUNK), 1)).astype(F32).astype(BF)
    return seq_of, char_of, pick_char, pick_seq


def side_masks():
    left = (iota((GROWS, KPAD), 1) < HEAD).astype(F32)
    return left.astype(BF), (1.0 - left).astype(BF)


def blocks(qkv, masks, group, pair, part):
    lanes = part * (qkv.shape[1] // 3) + pair * KPAD
    both = qkv[group * GROWS : (group + 1) * GROWS, lanes : lanes + KPAD]
    return jnp.concatenate([both * masks[0], both * masks[1]], axis=0)


def wide(rows, layer):
    pack, first = rows
    return pack[first + layer : first + layer + 1, :]


def small_rows(pack, layers, pieces):
    firsts = dict(g1=0, b1=layers, g2=2 * layers, b2=3 * layers, eb=4 * layers, embed=(4 + pieces) * layers)
    return SimpleNamespace(**{name: (pack, first) for name, first in firsts.items()})


EARLY = ("unit1", "rstd1", "norm1", "qkv", "probs")
KEPT = ("unit1", "rstd1", "norm1", "qkv", "probs", "att", "unit2", "rstd2", "norm2", "hid", "slp")


def kept_shapes(width, inner):
    row = {"rstd1": (KPAD, F32), "rstd2": (KPAD, F32), "qkv": (3 * width, BF), "hid": (inner, BF), "slp": (inner, BF)}
    shapes = {name: ((NROWS, row.get(name, (width, BF))[0]), row.get(name, (width, BF))[1]) for name in KEPT}
    shapes["probs"] = ((NGROUPS, HEADS // 2, 2 * GROWS, GROWS), BF)
    return [shapes[name] for name in KEPT]


def halves(size=HALF):
    return [slice(start, start + size) for start in range(0, NROWS, size)]


def strips(span, rows):
    return [slice(start, start + rows) for start in range(span.start, span.stop, rows)]


def groups_of(span):
    return range(span.start // GROWS, span.stop // GROWS)


def forward_tasks(layer, small, weight, kept, source, xs, mid, bias, masks, need, shifted=None):
    width = xs.shape[1]
    inner = kept.hid.shape[1]
    pairs = width // KPAD

    def normed(span, values, unit_ref, rstd_ref, norm_ref, gain, shift):
        unit, rstd = normalise(values[span, :])
        unit_ref[span, :] = unit.astype(BF)
        rstd_ref[span, :] = jnp.broadcast_to(rstd, (rstd.shape[0], KPAD))
        norm_ref[span, :] = (unit * wide(gain, layer) + wide(shift, layer)).astype(BF)

    def ln1(span):
        normed(span, source, kept.unit1, kept.rstd1, kept.norm1, small.g1, small.b1)

    def qkv(span):
        need("q")
        for part in range(3):
            lanes = slice(part * width, (part + 1) * width)
            product = nn(kept.norm1[span, :], weight.q[:, lanes])
            kept.qkv[span, lanes] = (product * 0.125 if part == 0 else product).astype(BF)

    def attend(span):
        for group in groups_of(span):
            rows = slice(group * GROWS, (group + 1) * GROWS)
            lanes = [slice(pair * KPAD, (pair + 1) * KPAD) for pair in range(pairs)]
            scores = [
                nt(blocks(kept.qkv, masks, group, pair, 1), kept.qkv[rows, lanes[pair]]) for pair in range(pairs)
            ]
            yield
            for pair in range(pairs):
                for side in range(2):
                    keys = slice(side * GROWS, (side + 1) * GROWS)
                    score = scores[pair][keys] + bias[group]
                    heft = jnp.exp(score - jnp.max(score, axis=0, keepdims=True))
                    prob = heft * (1.0 / jnp.sum(heft, axis=0, keepdims=True))
                    kept.probs[group, pair, keys, :] = prob.astype(BF)
            yield
            for pair in range(pairs):
                kept.att[rows, lanes[pair]] = tn(
                    kept.probs[group, pair], blocks(kept.qkv, masks, group, pair, 2)
                ).astype(BF)
            yield

    def out(span):
        need("o")
        mid[span, :] = source[span, :] + nn(kept.att[span, :], weight.o[...])

    def ln2(span):
        normed(span, mid, kept.unit2, kept.rstd2, kept.norm2, small.g2, small.b2)

    def up(span):
        need("e")
        for piece in range(inner // PIECE):
            cols = slice(piece * PIECE, (piece + 1) * PIECE)
            product = nn(kept.norm2[span, :], weight.e[:, cols])
            shift = wide(small.eb, layer * (inner // PIECE) + piece)
            for rows in strips(span, GSTRIP):
                strip = product[rows.start - span.start : rows.stop - span.start]
                hidden, slope = gelu_and_slope(strip + shift)
                kept.hid[rows, cols] = hidden.astype(BF)
                kept.slp[rows, cols] = slope.astype(BF)
                yield

    def down(span):
        need("c")
        for start in range(0, width, WIDE):
            cols = slice(start, start + WIDE)
            total = mid[span, cols] + nn(kept.hid[span, :], weight.c[:, cols])
            xs[span, cols] = total if shifted is None else total + shifted[span, cols]
            yield

    parts = dict(ln1=ln1, qkv=qkv, attend=attend, out=out, ln2=ln2, up=up, down=down)
    return {
        f"{name}{half}": (lambda part=part, span=span: part(span))
        for name, part in parts.items()
        for half, span in enumerate(halves())
    }


def backward_tasks(layer, small, weight, kept, work, masks, need, send, features, picks, grads):
    xs, mid, acc = work.xs, work.mid, work.acc
    width = xs.shape[1]
    inner = kept.hid.shape[1]
    pairs = width // KPAD
    left_lanes = iota((GROWS, KPAD), 1) < HEAD

    def add_rows(ref, span, value, cols=slice(None)):
        total = jnp.sum(value, axis=0, keepdims=True)
        ref[layer : layer + 1, cols] = total if span.start == 0 else ref[layer : layer + 1, cols] + total

    def grad_up(span):
        need("c", "slp")
        for piece in range(inner // PIECE):
            cols = slice(piece * PIECE, (piece + 1) * PIECE)
            value = nt(work.gff[span, :], weight.c[cols, :]) * kept.slp[span, cols].astype(F32)
            add_rows(grads.ub, span, value, cols)
            work.gu[span, cols] = value.astype(BF)

    def grad_norm2(span):
        need("e")
        acc[span, :] = nt(work.gu[span, :], weight.e[...])

    def ln2_back(span):
        need("unit2", "rstd2")
        for rows in strips(span, NSTRIP):
            unit, grad = kept.unit2[rows, :].astype(F32), acc[rows, :]
            add_rows(grads.g2, rows, grad * unit)
            add_rows(grads.b2, rows, grad)
            total = xs[rows, :] + norm_back(grad, unit, kept.rstd2[rows, 0:1], wide(small.g2, layer))
            mid[rows, :] = total
            work.gb[rows, :] = total.astype(BF)
            yield

    def grad_att(span):
        need("o")
        work.ga[span, :] = nt(work.gb[span, :], weight.o[...]).astype(BF)

    def attend_back(span):
        need("qkv", "probs")
        for group in groups_of(span):
            rows = slice(group * GROWS, (group + 1) * GROWS)
            lanes = [slice(pair * KPAD, (pair + 1) * KPAD) for pair in range(pairs)]
            grad_probs = [
                nt(blocks(kept.qkv, masks, group, pair, 2), work.ga[rows, lanes[pair]]) for pair in range(pairs)
            ]
            yield
            for pair in range(pairs):
                for side in range(2):
                    keys = slice(side * GROWS, (side + 1) * GROWS)
                    prob = kept.probs[group, pair, keys, :].astype(F32)
                    grad_prob = grad_probs[pair][keys]
                    delta = jnp.sum(prob * grad_prob, axis=0, keepdims=True)
                    work.gscore[pair, keys, :] = (prob * (grad_prob - delta)).astype(BF)
            yield
            for pair in range(pairs):
                grad_score = work.gscore[pair]
                work.gproj[rows, lanes[pair]] = (
                    tn(grad_score, blocks(kept.qkv, masks, group, pair, 1)) * 0.125
                ).astype(BF)
                grad_key = nn(grad_score, kept.qkv[rows, lanes[pair]])
                grad_value = nn(kept.probs[group, pair], work.ga[rows, lanes[pair]])
                for part, product in ((1, grad_key), (2, grad_value)):
                    joined = jnp.where(left_lanes, product[0:GROWS], product[GROWS : 2 * GROWS])
                    start = part * width + pair * KPAD
                    work.gproj[rows, start : start + KPAD] = joined.astype(BF)
            yield

    def grad_norm1(span):
        need("q")
        acc[span, :] = nt(work.gproj[span, :], weight.q[...])

    def ln1_back(span):
        need("unit1", "rstd1")
        for rows in strips(span, NSTRIP):
            unit, grad = kept.unit1[rows, :].astype(F32), acc[rows, :]
            add_rows(grads.g1, rows, grad * unit)
            add_rows(grads.b1, rows, grad)
            total = mid[rows, :] + norm_back(grad, unit, kept.rstd1[rows, 0:1], wide(small.g1, layer))
            xs[rows, :] = total
            work.gff[rows, :] = total.astype(BF)
            yield

    def down_term():
        need("hid")
        yield from send("down", layer, kept.hid, work.gff)

    def up_term():
        need("norm2")
        yield from send("up", layer, kept.norm2, work.gu)

    def out_term():
        need("att")
        yield from send("out", layer, kept.att, work.gb)

    def qkv_term():
        need("norm1")
        yield from send("qkv", layer, kept.norm1, work.gproj)

    def time_term():
        pick_char, pick_seq = picks
        by_seq = tn(pick_seq, work.gff[...]).astype(BF)
        yield from send("time", layer, features, by_seq)
        if layer == 0:
            grads.eg[...] = tn(pick_char, work.gff[...])[0 : grads.eg.shape[0]]

    by_half = dict(
        grad_up=grad_up, grad_norm2=grad_norm2, ln2_back=ln2_back, grad_att=grad_att,
        attend_back=attend_back, grad_norm1=grad_norm1, ln1_back=ln1_back,
    )
    tasks = {
        f"{name}{half}": (lambda part=part, span=span: part(span))
        for name, part in by_half.items()
        for half, span in enumerate(halves(NROWS))
    }
    tasks.update(down_term=down_term, up_term=up_term, out_term=out_term, qkv_term=qkv_term, time_term=time_term)
    return tasks


FIRST_ORDER = (
    "ln10", "ln11", "qkv0", "qkv1", "attend0", "attend1", "out0", "out1", "shift0", "ln20", "ln21", "up0", "up1",
    "down0", "down1",
)
SECOND_ORDER = ("ln10", "ln11", "qkv0", "qkv1", "attend0", "attend1")
LATTER_ORDER = ("out0", "out1", "ln20", "ln21", "up0", "down0|up1", "down1")
FORWARD_ORDER = (
    "ln10", "ln11", "qkv0", "qkv1", "attend0", "out0", "ln20", "attend1|up0", "out1", "ln21", "down0|up1", "down1",
)
BACKWARD_ORDER = (
    "grad_up0", "down_term", "grad_norm20", "ln2_back0|up_term", "grad_att0", "attend_back0|out_term", "grad_norm10",
    "ln1_back0|qkv_term", "time_term",
)


def bring(sources, targets, sems):
    copies = [pltpu.make_async_copy(a, b, sems.at[i]) for i, (a, b) in enumerate(zip(sources, targets))]
    for copy in copies:
        copy.start()
    return copies


def run_parts(names, tasks):
    steps = [step for step in (tasks[name]() for name in names.split("|")) if step is not None]
    while steps:
        steps = [step for step in steps if next(step, steps) is not steps]


def run_tasks(order, tasks, loads):
    for names in order:
        run_parts(names, tasks)
        loads.advance(PER_TASK)


def time_shift(features, weight, pick_seq):
    return nn(jnp.concatenate([pick_seq, pick_seq], axis=1), jnp.concatenate(hi_lo(nn(features, weight)), axis=0))


def first_layer(
    counts_ref, pack_ref,
    wt_hbm, wq_hbm, wo_hbm, we_hbm, wc_hbm,
    feat_ref, xs, next_att, next_o, *rest, vocab
):
    count = len(KEPT)
    kept_hbm, early_hbm, rest = rest[:count], rest[count : count + len(EARLY)], rest[count + len(EARLY) :]
    weight = SimpleNamespace(**dict(zip("tqoec", rest[:5])))
    kept_refs, rest = rest[5 : 5 + count], rest[5 + count :]
    kept = SimpleNamespace(**dict(zip(KEPT, kept_refs)))
    early_refs, rest = rest[: len(EARLY)], rest[len(EARLY) :]
    early = SimpleNamespace(att=next_att, hid=kept.hid, **dict(zip(EARLY, early_refs)))
    later, next_q, bias, mid, shifted, in_sem, out_sem, early_sem = rest
    width = xs.shape[1]
    small = small_rows(pack_ref, wt_hbm.shape[0], kept.hid.shape[1] // PIECE)
    loads = Loads(2)
    for index, (name, source) in enumerate(zip("tqoec", (wt_hbm, wq_hbm, wo_hbm, we_hbm, wc_hbm))):
        loads.add(name, source.at[0], getattr(weight, name), in_sem.at[index])
        if name == "o":
            loads.add("later", wt_hbm.at[1], later, in_sem.at[5])
    loads.add("next_q", wq_hbm.at[1], next_q, in_sem.at[6])
    loads.add("next_o", wo_hbm.at[1], next_o, in_sem.at[7])
    loads.begin()
    pushed = []

    def push(half, names, sources, targets, sems, wanted):
        for name in wanted:
            index = names.index(name)
            unit = GROWS if name == "probs" else 1
            rows = pl.ds(half * HALF // unit, HALF // unit)
            pushed.append(
                pltpu.make_async_copy(sources[index].at[rows], targets[index].at[rows], sems.at[index, half])
            )
            pushed[-1].start()

    _, _, pick_char, pick_seq = row_choices()
    masks = side_masks()

    shares = counts_ref.shape[0] // CHUNK
    stamp = []
    for group in range(NGROUPS):
        total = jnp.zeros((1, KPAD), F32)
        for member in range(GROUP):
            value = jnp.zeros((1, KPAD), F32)
            for share in range(shares):
                value = value + counts_ref[(group * GROUP + member) * shares + share]
            total = total + value
            stamp.append(jnp.broadcast_to(value[:, GROWS : GROWS + 1], (1, KPAD)))
        same = row_seq(iota((GROWS, GROWS), 1)) == row_seq(iota((GROWS, GROWS), 0))
        counts = jnp.broadcast_to(total[:, 0:GROWS], (GROWS, GROWS)).T
        live = same & (counts > 0.5)
        bias[group] = jnp.where(live, jnp.log(jnp.maximum(counts, 1.0)), MASKED)
    times = jnp.concatenate(stamp, axis=0)
    half = width // 2
    cycles = [
        times * jnp.exp((iota((1, KPAD), 1) + start).astype(F32) * (-math.log(10000.0) / half))
        for start in range(0, half, KPAD)
    ]
    features = jnp.concatenate(
        [jnp.sin(phase) for phase in cycles] + [jnp.cos(phase) for phase in cycles], axis=1
    ).astype(BF)
    feat_ref[...] = features
    loads.need("t")
    embed = pack_ref[small.embed[1] : small.embed[1] + vocab, :].astype(BF)
    xs[...] = nn(pick_char[:, 0:vocab], embed) + time_shift(features, weight.t[...], pick_seq)
    tasks = forward_tasks(0, small, weight, kept, xs, xs, mid, bias, masks, loads.need, shifted)

    def shift_next():
        loads.need("later")
        shifted[...] = time_shift(features, later[...], pick_seq)

    tasks["shift0"] = shift_next
    after = {"ln1": ("unit1", "rstd1", "norm1"), "qkv": ("qkv",), "attend": ("probs", "att"),
             "ln2": ("unit2", "rstd2", "norm2"), "up": ("hid", "slp")}
    second = forward_tasks(
        1, small, SimpleNamespace(q=next_q, o=next_o), early, xs, xs, mid, bias, masks,
        lambda name: loads.need("next_" + name),
    )
    for order, work, target in (
        (FIRST_ORDER, tasks, (KEPT, kept_refs, kept_hbm, out_sem)),
        (SECOND_ORDER, second, (EARLY, early_refs, early_hbm, early_sem)),
    ):
        for names in order:
            run_parts(names, work)
            loads.advance(PER_TASK)
            for name in names.split("|"):
                wanted = [array for array in after.get(name[:-1], ()) if array in target[0]]
                push(int(name[-1]), *target, wanted)
    loads.need("next_o")
    for copy in pushed:
        copy.wait()


def other_layers(
    own_ref, feat_ref, x_ref, att_ref, o_ref, pack_ref, chars_hbm,
    table_hbm, wt_hbm, wq_hbm, wo_hbm, we_hbm, wc_hbm, *rest, scale
):
    count = len(KEPT)
    layers, width = wq_hbm.shape[:2]
    kept_hbm, early_hbm, rest = rest[:count], rest[count : count + len(EARLY)], rest[count + len(EARLY) :]
    act_hbm, *little_hbm = rest[:7]
    outs = dict(zip(("time", "qkv", "out", "up", "down"), rest[7:12]))
    rest = rest[12:]
    weights, kept = [], []
    for layer in range(layers):
        weights.append(SimpleNamespace(**dict(zip("tqoec", rest[:5]))))
        kept.append(SimpleNamespace(**dict(zip(KEPT, rest[5 : 5 + count]))))
        rest = rest[5 + count :]
    weights[1].o, kept[1].att = o_ref, att_ref
    names = ("xs", "mid", "acc", "ga", "gproj", "gscore", "gu", "gb", "gff", "end", "act", "table")
    work = SimpleNamespace(**dict(zip(names, rest)))
    rest = rest[len(names) :]
    stages = dict(zip(outs, rest[:5]))
    little, rest = rest[5:11], rest[11:]
    chars_ref, rest = rest[0], rest[1:]
    in_sem, kept_sem, early_sem, out_sem, end_sem, small_sem, little_sem = rest
    eg, g1g, b1g, g2g, b2g, ubg = little
    xs, mid = work.xs, work.mid
    small = small_rows(pack_ref, layers, kept[0].hid.shape[1] // PIECE)
    (chars_copy,) = bring((chars_hbm,), (chars_ref,), small_sem)
    grads = SimpleNamespace(eg=eg, g1=g1g, b1=b1g, g2=g2g, b2=b2g, ub=ubg)
    sources = dict(zip("tqoec", (wt_hbm, wq_hbm, wo_hbm, we_hbm, wc_hbm)))
    loads = Loads(DEPTH)
    for layer in range(1, layers):
        for name in "ec" if layer == 1 else "tqoec":
            loads.add(
                (layer, name), sources[name].at[layer], getattr(weights[layer], name), in_sem.at["tqoec".index(name), layer]
            )
    for name in ("probs", "qkv", "norm1", "q", "unit1", "rstd1"):
        if name in EARLY:
            index = EARLY.index(name)
            loads.add((1, name), early_hbm[index], getattr(kept[1], name), early_sem.at[index])
        else:
            loads.add((1, name), sources[name].at[1], weights[1].q, in_sem.at["tqoec".index(name), 1])
    for name in ("slp", "c", "hid", "e", "norm2", "unit2", "rstd2", "o", "att", "probs", "qkv", "q", "norm1", "unit1", "rstd1"):
        if name in KEPT:
            index = KEPT.index(name)
            loads.add((0, name), kept_hbm[index], getattr(kept[0], name), kept_sem.at[index])
        else:
            loads.add((0, name), sources[name].at[0], getattr(weights[0], name), in_sem.at["tqoec".index(name), 0])
    loads.begin()
    table_copy = pltpu.make_async_copy(table_hbm, work.table, end_sem.at[2])
    table_copy.start()
    queued = {key for key, _ in loads.queue}

    def needs(layer):
        return lambda *names: loads.need(*((layer, name) for name in names if (layer, name) in queued))

    seq_of, char_of, pick_char, pick_seq = row_choices()
    masks = side_masks()
    features = feat_ref[...]
    for layer in range(1, layers):
        source, order = (x_ref, LATTER_ORDER) if layer == 1 else (xs, FORWARD_ORDER)
        if layer > 1:
            needs(layer)("t")
            xs[...] = xs[...] + time_shift(features, weights[layer].t[...], pick_seq)
        run_tasks(
            order,
            forward_tasks(layer, small, weights[layer], kept[layer], source, xs, mid, None, masks, needs(layer)),
            loads,
        )

    own = own_ref[0]
    work.end[0:NROWS, :] = xs[...].astype(BF)
    work.end[NROWS:, :] = jnp.zeros((work.end.shape[0] - NROWS, width), BF)
    chars_copy.wait()
    place = chars_ref[...] + lax.rem(own, GROUP) * ROWS
    hot = (place == iota((KPAD, chars_ref.shape[1]), 0)).astype(F32).astype(BF)
    start = pl.multiple_of(lax.div(own, GROUP) * GROWS, 16)
    work.act[...] = tn(hot, work.end[pl.ds(start, KPAD), :]).astype(BF)
    act_copy = pltpu.make_async_copy(work.act, act_hbm, end_sem.at[1])
    act_copy.start()

    table_copy.wait()
    for seq in range(CHUNK):
        xs[seq * ROWS : (seq + 1) * ROWS, :] = work.table[seq].astype(F32)[0:ROWS] * scale
    work.gff[...] = xs[...].astype(BF)

    sends = {}

    def send(name, layer, left, right):
        if name in sends:
            sends.pop(name).wait()
        stage = stages[name]
        for start in range(0, stage.shape[0], BAND):
            stage[start : start + BAND, :] = tn(left[:, start : start + BAND], right[...])
            yield
        copy = pltpu.make_async_copy(stage, outs[name].at[layer], out_sem.at[list(outs).index(name), layer])
        copy.start()
        sends[name] = copy

    for layer in reversed(range(layers)):
        run_tasks(
            BACKWARD_ORDER,
            backward_tasks(layer, small, weights[layer], kept[layer], work, masks, needs(layer), send,
                           features, (pick_char, pick_seq), grads),
            loads,
        )
    finals = bring(little, little_hbm, little_sem)
    act_copy.wait()
    for copy in [*sends.values(), *finals]:
        copy.wait()


def vmem():
    return pl.BlockSpec(memory_space=pltpu.VMEM)


def smem():
    return pl.BlockSpec(memory_space=pltpu.SMEM)


def anywhere():
    return pl.BlockSpec(memory_space=pl.ANY)


def call(body, outs, ins, in_specs, out_specs, scratch=(), name=None, mib=8):
    return pl.pallas_call(
        body,
        out_shape=outs,
        in_specs=in_specs,
        out_specs=out_specs,
        scratch_shapes=list(scratch),
        compiler_params=pltpu.CompilerParams(vmem_limit_bytes=mib * MIB),
        name=name,
    )(*ins)


def far(array):
    return pltpu.with_memory_space_constraint(array, pltpu.HBM)


def keep(array):
    return pltpu.with_memory_space_constraint(array, pltpu.VMEM)


def run_forward(counts, pack, weights, big):
    embed, expand_bias = weights[0], weights[9]
    width, inner = embed.shape[1], expand_bias.shape[1]
    shapes = kept_shapes(width, inner)
    early = [shapes[KEPT.index(name)] for name in EARLY]
    table = (NROWS, width)
    return call(
        lambda *refs: first_layer(*refs, vocab=embed.shape[0]),
        [
            pltpu.VMEM((CHUNK, width), BF),
            pltpu.VMEM(table, F32),
            pltpu.VMEM(table, BF),
            pltpu.VMEM(big[2].shape[1:], BF),
        ]
        + [pltpu.HBM(shape, dtype) for shape, dtype in shapes + early],
        (counts, keep(pack), *map(far, big)),
        [vmem()] * 2 + [anywhere()] * len(big),
        [vmem()] * 4 + [anywhere()] * (len(shapes) + len(early)),
        [pltpu.VMEM(w.shape[1:], w.dtype) for w in big]
        + [pltpu.VMEM(shape, dtype) for shape, dtype in shapes + early]
        + [
            pltpu.VMEM(big[0].shape[1:], BF),
            pltpu.VMEM(big[1].shape[1:], BF),
            pltpu.VMEM((NGROUPS, GROWS, GROWS), F32),
            pltpu.VMEM(table, F32),
            pltpu.VMEM(table, F32),
            pltpu.SemaphoreType.DMA((len(big) + 3,)),
            pltpu.SemaphoreType.DMA((len(shapes), NROWS // HALF)),
            pltpu.SemaphoreType.DMA((len(early), NROWS // HALF)),
        ],
        name="forward",
        mib=40,
    )


def run_backward(own, chars_row, pack, table, weights, big, passed, scale):
    (embed, ln1_gain, ln1_bias, w_time, w_qkv, w_out, ln2_gain, ln2_bias, expand_weight, expand_bias,
     contract_weight) = weights
    layers, width = ln1_gain.shape
    inner = expand_bias.shape[1]
    shapes = kept_shapes(width, inner)
    positions = chars_row.shape[1]
    whole = (NROWS, width)

    def f32_like(array):
        return jax.ShapeDtypeStruct(array.shape, F32)

    features, x, att, next_o, *kept = passed
    layer_scratch = [pltpu.VMEM(w.shape[1:], w.dtype) for w in big] + [
        pltpu.VMEM(shape, dtype) for shape, dtype in shapes
    ]
    smalls = (ln1_gain, ln1_bias, ln2_gain, ln2_bias, expand_bias)
    little = (embed, *smalls)
    outs = call(
        lambda *refs: other_layers(*refs, scale=scale),
        [jax.ShapeDtypeStruct((positions, width), BF)]
        + [f32_like(w) for w in (*little, w_time, w_qkv, w_out, expand_weight, contract_weight)],
        (own, keep(features), keep(x), keep(att), keep(next_o), keep(pack), far(chars_row), keep(table), *map(far, big),
         *map(far, kept)),
        [smem()] + [vmem()] * 5 + [anywhere()] * (2 + len(big) + len(kept)),
        [anywhere()] * 12,
        layer_scratch * layers
        + [
            pltpu.VMEM(whole, F32),
            pltpu.VMEM(whole, F32),
            pltpu.VMEM(whole, F32),
            pltpu.VMEM(whole, BF),
            pltpu.VMEM((NROWS, 3 * width), BF),
            pltpu.VMEM((HEADS // 2, 2 * GROWS, GROWS), BF),
            pltpu.VMEM((NROWS, inner), BF),
            pltpu.VMEM(whole, BF),
            pltpu.VMEM(whole, BF),
            pltpu.VMEM((NROWS + KPAD - GROWS, width), BF),
            pltpu.VMEM((positions, width), BF),
            pltpu.VMEM(table.shape, BF),
        ]
        + [pltpu.VMEM(w.shape[1:], F32) for w in big]
        + [pltpu.VMEM(w.shape, F32) for w in little]
        + [pltpu.VMEM(chars_row.shape, I32)]
        + [
            pltpu.SemaphoreType.DMA((len(big), layers)),
            pltpu.SemaphoreType.DMA((len(shapes),)),
            pltpu.SemaphoreType.DMA((len(EARLY),)),
            pltpu.SemaphoreType.DMA((len(big), layers)),
            pltpu.SemaphoreType.DMA((3,)),
            pltpu.SemaphoreType.DMA((1,)),
            pltpu.SemaphoreType.DMA((len(little),)),
        ],
        name="backward",
        mib=60,
    )
    act, eg, g1, b1, g2, b2, ub, tg, qg, og, ug, dg = outs
    return act, (eg, g1, b1, tg, qg, og, g2, b2, ug, ub, dg)


def per_device(chars, timesteps, *rest):
    weights, cotangent = rest[:-1], rest[-1]
    width = weights[0].shape[1]
    n_dp, n_blk = lax.axis_size("dp"), lax.axis_size("blk")
    seq = lax.axis_index("dp")
    positions = chars.shape[0]
    chars_row = chars.reshape(1, positions)
    big = [weights[i] for i in (3, 4, 5, 8, 10)]
    counts, sums = call(
        lambda *refs: local_sums(*refs, shares=n_blk),
        [
            pltpu.VMEM((n_dp * n_blk, 1, KPAD), F32),
            pltpu.VMEM((SLOT, width), F32),
        ],
        (
            far(chars_row),
            far(cotangent.reshape(positions, width)),
            (seq % GROUP).astype(I32).reshape(1),
            timesteps,
        ),
        [vmem(), vmem(), smem(), smem()],
        [vmem(), vmem()],
        name="local_sums",
    )
    counts = lax.all_to_all(counts, ("dp", "blk"), split_axis=0, concat_axis=0, tiled=True)
    parts = [sums] + [
        lax.ppermute(sums, "blk", [(i, (i + step) % n_blk) for i in range(n_blk)])
        for step in range(1, n_blk)
    ]
    embed, ln1_gain, ln1_bias, _, _, _, ln2_gain, ln2_bias, _, expand_bias, _ = weights
    smalls = (embed, ln1_gain, ln1_bias, ln2_gain, ln2_bias, expand_bias)
    pack_rows = sum(w.size for w in smalls) // width
    table, pack = call(
        spread_sums,
        [
            pltpu.VMEM((n_dp, SLOT, width), BF) if n_dp == CHUNK else jax.ShapeDtypeStruct((n_dp, SLOT, width), BF),
            pltpu.VMEM((pack_rows + -pack_rows % 8, width), F32),
        ],
        (*parts, *map(far, smalls)),
        [vmem()] * (len(parts) + len(smalls)),
        [vmem()] * 2,
        name="spread_sums",
    )
    table = lax.all_to_all(table, "dp", split_axis=0, concat_axis=0, tiled=True)
    scale = 1.0 / (n_dp * n_blk)
    if n_dp == CHUNK:
        kept = run_forward(counts, pack, weights, big)
        act, grads = run_backward(seq.reshape(1).astype(I32), chars_row, pack, table, weights, big, kept, scale)
    else:

        def step(carry, chunk):
            act, grads = carry
            place = seq - chunk * CHUNK
            inside = (place >= 0) & (place < CHUNK)
            here = lax.dynamic_slice_in_dim(counts, chunk * CHUNK * n_blk, CHUNK * n_blk, axis=0)
            part = lax.dynamic_slice_in_dim(table, chunk * CHUNK, CHUNK, axis=0)
            own = jnp.clip(place, 0, CHUNK - 1).reshape(1).astype(I32)
            kept = run_forward(here, pack, weights, big)
            new_act, new_grads = run_backward(own, chars_row, pack, part, weights, big, kept, scale)
            return (jnp.where(inside, new_act, act), tuple(a + b for a, b in zip(grads, new_grads))), None

        start = (jnp.zeros((positions, width), BF), tuple(jnp.zeros(w.shape, F32) for w in weights))
        (act, grads), _ = lax.scan(step, start, jnp.arange(n_dp // CHUNK, dtype=I32))
    return (act.reshape(positions, 1, width), *grads)


def solution(mesh):
    in_specs = (P("blk", "dp"), P("dp")) + (P(),) * 11 + (P("blk", "dp", None),)
    out_specs = (P("blk", "dp", None),) + (P(),) * 11
    return jax.shard_map(
        per_device, mesh=mesh, in_specs=in_specs, out_specs=out_specs, check_vma=False
    )
```
